256 devices in a mesh: section: 4 (over x), seq: 8 (over y, core), tensor: 8 (over z).
Axes of the slice: x: 4, y: 4, z: 8, core: 2. Of those that a mesh axis runs over, the one named last changes fastest.
Arguments:
- prompt_query: bfloat16 [4, 4096, 8192], P('section', 'seq', 'tensor'), may hold values from -137 to 137
- prompt_keys: bfloat16 [4, 4096, 1024], P('section', 'seq', 'tensor'), may hold values from -4.6 to 4.6
- prompt_values: bfloat16 [4, 4096, 1024], P('section', 'seq', 'tensor'), may hold values from -6 to 6
- page_owner: int32 [4, 128], P('section', 'seq'), may hold values from 0 to 31, as said below
- pool_keys: bfloat16 [8192, 32, 1024], P(('section', 'seq'), None, 'tensor'), may hold values from -4.6 to 4.6
- pool_values: bfloat16 [8192, 32, 1024], P(('section', 'seq'), None, 'tensor'), may hold values from -6 to 6
- step_query: bfloat16 [512, 4, 8192], P(('section', 'seq'), None, 'tensor'), may hold values from -137 to 137
- step_keys: bfloat16 [512, 4, 1024], P(('section', 'seq'), None, 'tensor'), may hold values from -4.5 to 4.5
- step_values: bfloat16 [512, 4, 1024], P(('section', 'seq'), None, 'tensor'), may hold values from -6 to 6
- page_table: int32 [512, 64], P(('section', 'seq')), may hold values from 0 to 287, as said below
- context_len: int32 [512], P(('section', 'seq')), may hold values from 2 to 2048, as said below
Outputs:
- prefill_out: bfloat16 [4, 4096, 8192], P('section', 'seq', 'tensor')
- decode_out: bfloat16 [512, 4, 8192], P(('section', 'seq'), None, 'tensor')
The draws below stay inside these ranges and needn't reach their ends.
Inputs may be any that keep to these rules, and one draw needn't show every extreme that they name: `page_owner`: no decode device takes more than 1 pages of one block; some decode device takes exactly 1 pages of every block. `page_table`: an entry 256 + b + k appears only where block b sends more than k pages to the request's decode device. Every entry, used or not, follows this rule. The first entry of every row is below 256. `context_len`: some request has exactly 2048 cached tokens.
All inputs are finite; a program needn't handle non-finite values.
Results may differ from the reference program's by a relative error of at most 0.0045.
Values may be sent and summed in bfloat16 or wider, within the bound.
A program may use at most 192 MiB of HBM per device.

```python
import math
import jax
import jax.numpy as jnp
from jax import lax

HEADS = 64
KV_HEADS = 8
HEAD_DIM = 128
PAGE = 32
REQ_DEV = 16
POOL = 256
MAXPG = 64
STEPS = 4
LEN = 4096
SEQS = 4
PG_DEV = 16
DECODERS = 32
CAP = 1
REQUESTS = 512
MAXCTX = 2048
POOL_ALL = 8192
PROMPT_PAGES = 512


def raw_prompt_keys(key):
    return jnp.clip(jax.random.normal(jax.random.fold_in(key, 101), (SEQS, LEN, KV_HEADS * HEAD_DIM), jnp.float32), -4.5, 4.5)


def raw_pool_keys(key):
    return jnp.clip(jax.random.normal(jax.random.fold_in(key, 102), (POOL_ALL, PAGE, KV_HEADS * HEAD_DIM), jnp.float32), -4.5, 4.5)


def raw_step_keys(key):
    return jnp.clip(jax.random.normal(jax.random.fold_in(key, 103), (REQUESTS, STEPS, KV_HEADS * HEAD_DIM), jnp.float32), -4.5, 4.5)


def spread_heads(array):
    shape = array.shape[:-1]
    grouped = array.reshape(shape + (KV_HEADS, 1, HEAD_DIM))
    wide = jnp.broadcast_to(grouped, shape + (KV_HEADS, HEADS // KV_HEADS, HEAD_DIM))
    return wide.reshape(shape + (HEADS * HEAD_DIM,))


def favored_device(key):
    first = jax.random.fold_in(jax.random.fold_in(key, 104), 0)
    return jax.random.randint(first, (), 0, DECODERS)


def assign_pages(key):
    base = jax.random.fold_in(key, 104)
    second = jax.random.fold_in(base, 1)
    third = jax.random.fold_in(base, 2)
    favored = favored_device(key)
    total_slots = CAP * DECODERS
    slots = jnp.arange(total_slots, dtype=jnp.int32)
    owner_of = slots % DECODERS
    noise = jax.random.randint(second, (DECODERS, total_slots), 0, 1 << 20)
    ranks = jnp.where((owner_of == favored)[None, :], slots[None, :], (noise + 1) * total_slots + slots[None, :])
    order = jnp.argsort(ranks, axis=1)[:, :PG_DEV]
    dests = owner_of[order]
    mixing = jax.random.randint(third, (DECODERS, PG_DEV), 0, 1 << 20) * PG_DEV + jnp.arange(PG_DEV, dtype=jnp.int32)[None, :]
    perm = jnp.argsort(mixing, axis=1)
    dests = jnp.take_along_axis(dests, perm, axis=1)
    return dests.reshape(SEQS, LEN // PAGE).astype(jnp.int32)


def tables(key):
    dests = assign_pages(key).reshape(DECODERS, PG_DEV)
    base = jax.random.fold_in(key, 105)
    first, second, third = jax.random.split(base, 3)
    counts_db = jnp.sum((dests[None, :, :] == jnp.arange(DECODERS)[:, None, None]).astype(jnp.int32), axis=2)
    received = (counts_db[:, :, None] > jnp.arange(CAP)[None, None, :]).reshape(DECODERS, DECODERS * CAP)
    order = jnp.argsort(jnp.where(received, 0, 1), axis=1, stable=True)
    counts = jnp.sum(received.astype(jnp.int32), axis=1)
    device = jnp.arange(REQUESTS) // REQ_DEV
    pick = jax.random.randint(first, (REQUESTS, MAXPG), 0, 1 << 20) % jnp.maximum(counts[device], 1)[:, None]
    source = order[device[:, None], pick]
    coin = jax.random.randint(second, (REQUESTS, MAXPG), 0, 2) == 1
    local = jax.random.randint(third, (REQUESTS, MAXPG), 0, POOL)
    column = jnp.arange(MAXPG)[None, :]
    chosen = coin & (counts[device] > 0)[:, None] & (column > 0)
    result = jnp.where(chosen, POOL + source, local).astype(jnp.int32)
    favored = favored_device(key)
    blocks = jnp.stack([(favored + DECODERS - 1) % DECODERS, (favored + 1) % DECODERS, (favored + DECODERS // 2) % DECODERS])
    planted = (POOL + blocks * CAP).astype(jnp.int32)
    return result.at[favored * REQ_DEV, 1:4].set(planted)


def draw_prompt_keys(key, part):
    keys = raw_prompt_keys(key)
    return keys.astype(jnp.bfloat16)


def draw_prompt_query(key, part):
    own = jax.random.fold_in(key, 2)
    first = jax.random.fold_in(own, 0)
    query = 2.5 * jnp.clip(jax.random.normal(first, (SEQS, LEN, HEADS * HEAD_DIM), jnp.float32), -6.0, 6.0)
    return query.astype(jnp.bfloat16)


def draw_page_owner(key, part):
    return assign_pages(key)


def draw_pool_keys(key, part):
    keys = raw_pool_keys(key)
    return keys.astype(jnp.bfloat16)


def draw_step_keys(key, part):
    return raw_step_keys(key).astype(jnp.bfloat16)


def draw_step_query(key, part):
    own = jax.random.fold_in(key, 6)
    first = jax.random.fold_in(own, 0)
    fresh = spread_heads(raw_step_keys(key))
    query = 2.5 * jnp.clip(jax.random.normal(first, (REQUESTS, STEPS, HEADS * HEAD_DIM), jnp.float32), -6.0, 6.0) + 0.8 * fresh
    return query.astype(jnp.bfloat16)


def draw_page_table(key, part):
    return tables(key)


def draw_context_len(key, part):
    own = jax.random.fold_in(key, 8)
    first, second = jax.random.split(own, 2)
    level = jax.random.randint(first, (DECODERS,), 1, 5)
    base = jax.random.randint(second, (REQUESTS,), 0, MAXCTX - 1)
    device = jnp.arange(REQUESTS) // REQ_DEV
    lengths = 2 + base * level[device] // 4
    longest = favored_device(key) * REQ_DEV
    return jnp.where(jnp.arange(REQUESTS) == longest, MAXCTX, lengths).astype(jnp.int32)


def levels(stream_key, extent, cuts, smallest, largest):
    def one(position, parts):
        draws = jax.random.uniform(jax.random.fold_in(jax.random.fold_in(stream_key, 6), position), (parts,), jnp.float32, smallest / len(cuts), largest / len(cuts))
        return jnp.repeat(jnp.exp(draws), extent[position] // parts).reshape((-1,) + (1,) * (len(extent) - position - 1))

    gain = one(*cuts[0])
    for cut in cuts[1:]:
        gain = gain * one(*cut)
    return gain


def centred(stream_key, extent, deviation, bound, cuts=(), kind=jnp.bfloat16):
    gain = levels(stream_key, extent, cuts, -0.22, 0.18) if cuts else 1.0
    values = jax.random.normal(stream_key, extent, jnp.float32) * deviation * gain
    return jnp.minimum(jnp.maximum(values, -bound), bound).astype(kind)


def setup_inputs(seed: int = 0) -> dict:
    splits = jax.random.split(jax.random.key(seed), 12)
    prompt_query = draw_prompt_query(jax.random.fold_in(splits[11], 71), 0)
    prompt_keys = draw_prompt_keys(jax.random.fold_in(splits[11], 71), 0)
    prompt_values = centred(splits[2], (SEQS, LEN, KV_HEADS * HEAD_DIM), 1.0, 6.0, ((0, 4), (1, 8), (2, 8)))
    page_owner = draw_page_owner(jax.random.fold_in(splits[11], 71), 0)
    pool_keys = draw_pool_keys(jax.random.fold_in(splits[11], 71), 0)
    pool_values = centred(splits[5], (POOL_ALL, PAGE, KV_HEADS * HEAD_DIM), 1.0, 6.0, ((0, 32), (2, 8)))
    step_query = draw_step_query(jax.random.fold_in(splits[11], 71), 0)
    step_keys = draw_step_keys(jax.random.fold_in(splits[11], 71), 0)
    step_values = centred(splits[8], (REQUESTS, STEPS, KV_HEADS * HEAD_DIM), 1.0, 6.0, ((0, 32), (2, 8)))
    page_table = draw_page_table(jax.random.fold_in(splits[11], 71), 0)
    context_len = draw_context_len(jax.random.fold_in(splits[11], 71), 0)
    return dict(prompt_query=prompt_query, prompt_keys=prompt_keys, prompt_values=prompt_values, page_owner=page_owner, pool_keys=pool_keys, pool_values=pool_values, step_query=step_query, step_keys=step_keys, step_values=step_values, page_table=page_table, context_len=context_len)


def attend_rows(scores, valid, values, pattern):
    masked = jnp.where(valid, scores, jnp.float32(-jnp.inf))
    top = lax.optimization_barrier(jnp.max(masked, axis=-1))
    weights = jnp.where(valid, jnp.exp(masked - top[..., None]), jnp.float32(0.0))
    total = lax.optimization_barrier(jnp.sum(weights, axis=-1))
    rounded = lax.optimization_barrier(weights.astype(jnp.bfloat16)).astype(jnp.float32)
    summed = jnp.einsum(pattern, rounded, values)
    return (summed / total[..., None]).astype(jnp.bfloat16)

def reference(prompt_query, prompt_keys, prompt_values, page_owner, pool_keys, pool_values, step_query, step_keys, step_values, page_table, context_len):
    group = HEADS // KV_HEADS
    scale = 1.0 / math.sqrt(HEAD_DIM)

    def one_sequence(item):
        query, keys, values = item
        qf = query.astype(jnp.float32).reshape(LEN, KV_HEADS, group, HEAD_DIM)
        kf = keys.astype(jnp.float32).reshape(LEN, KV_HEADS, HEAD_DIM)
        vf = values.astype(jnp.float32).reshape(LEN, KV_HEADS, HEAD_DIM)
        width = math.gcd(LEN, 128)

        def block(index):
            qb = lax.dynamic_slice_in_dim(qf, index * width, width, 0)
            scores = jnp.einsum('tkgd,skd->tkgs', qb, kf) * scale
            rows = index * width + jnp.arange(width, dtype=jnp.int32)
            valid = (jnp.arange(LEN, dtype=jnp.int32)[None, :] <= rows[:, None])[:, None, None, :]
            return attend_rows(scores, valid, vf, 'tkgs,skd->tkgd')
        return lax.map(block, jnp.arange(LEN // width, dtype=jnp.int32)).reshape(LEN, HEADS * HEAD_DIM)
    prefill_out = lax.map(one_sequence, (prompt_query, prompt_keys, prompt_values))
    page_keys = prompt_keys.reshape(PROMPT_PAGES, PAGE, KV_HEADS * HEAD_DIM)
    page_values = prompt_values.reshape(PROMPT_PAGES, PAGE, KV_HEADS * HEAD_DIM)
    destinations = page_owner.reshape(DECODERS, PG_DEV)

    def one_request(row):
        device = row // REQ_DEV
        entry = page_table[row]
        in_pool = entry < POOL
        pool_index = device * POOL + jnp.where(in_pool, entry, 0)
        slot_all = jnp.where(in_pool, 0, entry - POOL).astype(jnp.int32)
        source = (slot_all // CAP).astype(jnp.int32)
        order_k = (slot_all % CAP).astype(jnp.int32)
        owned = destinations[source] == device
        ranks = jnp.cumsum(owned.astype(jnp.int32), axis=1).astype(jnp.int32) - 1
        hit = owned & (ranks == order_k[:, None])
        slot = lax.optimization_barrier(jnp.sum(jnp.where(hit, jnp.arange(PG_DEV, dtype=jnp.int32)[None, :], 0), axis=1)).astype(jnp.int32)
        page_index = (source * PG_DEV + slot).astype(jnp.int32)
        keys = jnp.where(in_pool[:, None, None], pool_keys[pool_index], page_keys[page_index])
        values = jnp.where(in_pool[:, None, None], pool_values[pool_index], page_values[page_index])
        keys = jnp.concatenate([keys.reshape(MAXCTX, KV_HEADS * HEAD_DIM), step_keys[row]], 0)
        values = jnp.concatenate([values.reshape(MAXCTX, KV_HEADS * HEAD_DIM), step_values[row]], 0)
        kf = keys.astype(jnp.float32).reshape(MAXCTX + STEPS, KV_HEADS, HEAD_DIM)
        vf = values.astype(jnp.float32).reshape(MAXCTX + STEPS, KV_HEADS, HEAD_DIM)
        qf = step_query[row].astype(jnp.float32).reshape(STEPS, KV_HEADS, group, HEAD_DIM)
        scores = jnp.einsum('tkgd,skd->tkgs', qf, kf) * scale
        cols = jnp.arange(MAXCTX + STEPS, dtype=jnp.int32)
        steps_here = jnp.arange(STEPS, dtype=jnp.int32)
        valid = jnp.where(cols[None, :] < MAXCTX, cols[None, :] < context_len[row], cols[None, :] - MAXCTX <= steps_here[:, None])
        out = attend_rows(scores, valid[:, None, None, :], vf, 'tkgs,skd->tkgd')
        return out.reshape(STEPS, HEADS * HEAD_DIM)
    decode_out = lax.map(one_request, jnp.arange(REQUESTS, dtype=jnp.int32))
    return (prefill_out, decode_out)
```

```python
import functools
import math

import jax
import jax.numpy as jnp
from jax import lax
from jax.experimental import pallas as pl
from jax.experimental.pallas import tpu as pltpu
from jax.sharding import PartitionSpec as P

MESH = pl.DeviceIdType.MESH
HD = 128
PAGE = 32
MAXPG = 64
STEPS = 4
GROUP = 8
TOK = 512
VROWS = 144
POOL = 256
REQS = 16
CTX = MAXPG * PAGE
ROWS = STEPS * GROUP
SCALE = math.log2(math.e) / math.sqrt(HD)
LIMIT = 2.0**100
LOW = -1e30
NT = (((1,), (1,)), ((), ()))


def dot_nt(a, b):
    return lax.dot_general(a, b, NT, preferred_element_type=jnp.float32)


def dot_nn(a, b):
    return jnp.dot(a, b, preferred_element_type=jnp.float32)


def prefill_kernel(
    chips, sections,
    q_ref, k_ref, v_ref, owner_ref,
    out_ref, total_ref, karch_ref, varch_ref, arrived_ref,
    kall, vall, acc, shift, pages,
    ksend, vsend, krecv, vrecv, fksend, fvsend, psend, precv, asem,
):
    section = lax.axis_index("section")
    seq = lax.axis_index("seq")
    tensor = lax.axis_index("tensor")
    width = 2 * chips
    count = sections * width
    chip, core = seq // 2, seq % 2
    mate = chip * 2 + (1 - core)
    block = section * width + seq

    barrier = pltpu.get_barrier_semaphore()

    @pl.loop(1, count)
    def _(step):
        other = lax.rem(block + step, count)
        pl.semaphore_signal(
            barrier, inc=1,
            device_id=(other // width, lax.rem(other, width), tensor), device_id_type=MESH,
        )

    own_k = k_ref[...].reshape(TOK, HD)
    own_v = v_ref[...].reshape(TOK, HD)
    vall[seq, :HD, :] = own_v.T
    for index in range(width):
        vall[index, HD:, :] = jnp.ones((VROWS - HD, TOK), jnp.bfloat16)
    pl.semaphore_wait(barrier, count - 1)

    def k_copy(source, held, target, ssem):
        return pltpu.make_async_remote_copy(
            src_ref=source, dst_ref=kall.at[held], send_sem=ssem, recv_sem=krecv.at[held],
            device_id=(section, target, tensor), device_id_type=MESH,
        )

    def v_copy(held, target, ssem):
        return pltpu.make_async_remote_copy(
            src_ref=vall.at[held, pl.ds(0, HD)], dst_ref=vall.at[held, pl.ds(0, HD)],
            send_sem=ssem, recv_sem=vrecv.at[held],
            device_id=(section, target, tensor), device_id_type=MESH,
        )

    @pl.when(core == 0)
    def _():
        k_copy(k_ref, seq, mate, fksend.at[chip]).start()
        v_copy(seq, mate, fvsend.at[chip]).start()

    @pl.loop(chip + 1, chips)
    def _(far):
        target = far * 2 + core
        k_copy(k_ref, seq, target, ksend.at[far]).start()
        v_copy(seq, target, vsend.at[far]).start()

    def page_copy(step):
        other = lax.rem(block + step, count)
        return pltpu.make_async_remote_copy(
            src_ref=pages.at[other], dst_ref=arrived_ref.at[block],
            send_sem=psend.at[other], recv_sem=precv.at[block],
            device_id=(other // width, lax.rem(other, width), tensor), device_id_type=MESH,
        )

    def fill_page(target):
        place = jnp.int32(0)
        for page in range(TOK // PAGE):
            place = jnp.where(owner_ref[0, page] == target, page, place)
        pages[target, :PAGE, :] = k_ref[place]
        pages[target, PAGE:, :] = v_ref[place]

    fill_page(block)
    own_page = pltpu.make_async_copy(pages.at[block], arrived_ref.at[block], asem.at[0])
    own_page.start()

    @pl.loop(1, count)
    def _(step):
        fill_page(lax.rem(block + step, count))
        page_copy(step).start()

    ones = jnp.ones((8, HD), jnp.bfloat16)
    half = TOK // 2
    k_low, k_high = own_k[:half], own_k[half:]
    key_at = lax.broadcasted_iota(jnp.int32, (half, TOK), 0)
    query_at = lax.broadcasted_iota(jnp.int32, (half, TOK), 1)
    low_valid = key_at <= query_at
    high_valid = low_valid[:, :half]

    def query(head):
        return q_ref[0, :, head * HD:(head + 1) * HD]

    shifts = []
    for head in range(GROUP):
        product = (query(head).astype(jnp.float32) * own_k.astype(jnp.float32)).astype(jnp.bfloat16)
        shifts.append(dot_nt(ones, product)[:1])
    for head in range(GROUP):
        shift[head] = shifts[head]

    def own_scores(head):
        q = query(head)
        return dot_nt(k_low, q), dot_nt(k_high, q[half:])

    scores = own_scores(0)
    for head in range(GROUP):
        following = own_scores(head + 1) if head + 1 < GROUP else None
        base = shift[head]
        low = jnp.where(low_valid, jnp.exp2((scores[0] - base) * SCALE), 0.0)
        high = jnp.where(high_valid, jnp.exp2((scores[1] - base[:, half:]) * SCALE), 0.0)
        first = dot_nn(vall[seq, :, :half], low.astype(jnp.bfloat16))
        second = dot_nn(vall[seq, :, half:], high.astype(jnp.bfloat16))
        acc[head, :, :half] = first[:, :half]
        acc[head, :, half:] = first[:, half:] + second
        scores = following

    def attend(held_blocks):
        keys = jnp.concatenate([kall[b].reshape(TOK, HD) for b in held_blocks], axis=0)
        values = jnp.concatenate([vall[b] for b in held_blocks], axis=1)
        scores = dot_nt(keys, query(0))
        for head in range(GROUP):
            following = dot_nt(keys, query(head + 1)) if head + 1 < GROUP else None
            weights = jnp.exp2((scores - shift[head]) * SCALE).astype(jnp.bfloat16)
            acc[head] += dot_nn(values, weights)
            scores = following

    def archive(held):
        return (
            pltpu.make_async_copy(kall.at[held], karch_ref.at[held], asem.at[1 + 2 * held]),
            pltpu.make_async_copy(vall.at[held], varch_ref.at[held], asem.at[2 + 2 * held]),
        )

    kall[seq] = k_ref[...]
    for copy in archive(seq):
        copy.start()

    @pl.when(core == 1)
    def _():
        k_copy(k_ref, mate, seq, fksend.at[0]).wait_recv()
        v_copy(mate, seq, fvsend.at[0]).wait_recv()
        for copy in archive(mate):
            copy.start()
        attend([mate])

    def near_first(step):
        if chips == 4:
            order = jnp.where(chip == 3, jnp.where(step == 0, 2, jnp.where(step == 1, 0, 1)), chip - 1 - step)
        else:
            order = chip - 1 - step
        return order

    @pl.loop(0, chip)
    def _(step):
        far = near_first(step)
        direct = far * 2 + core
        passed = far * 2 + 1 - core
        k_copy(k_ref, direct, seq, ksend.at[0]).wait_recv()
        k_copy(kall.at[direct], direct, mate, fksend.at[far]).start()
        v_copy(direct, seq, vsend.at[0]).wait_recv()
        v_copy(direct, mate, fvsend.at[far]).start()
        for copy in archive(direct):
            copy.start()
        k_copy(k_ref, passed, seq, ksend.at[0]).wait_recv()
        v_copy(passed, seq, vsend.at[0]).wait_recv()
        for copy in archive(passed):
            copy.start()
        attend([direct, passed])

    for head in range(GROUP):
        state = acc[head]
        total = state[HD:HD + 1]
        total_ref[head:head + 1, :] = total
        out_ref[0, :, head * HD:(head + 1) * HD] = (state[:HD] / total).astype(jnp.bfloat16).T

    for copy in archive(seq):
        copy.wait()

    @pl.when(core == 1)
    def _():
        for copy in archive(mate):
            copy.wait()

    @pl.loop(0, chip)
    def _(far):
        for held in (far * 2, far * 2 + 1):
            for copy in archive(held):
                copy.wait()
        k_copy(k_ref, seq, mate, fksend.at[far]).wait_send()
        v_copy(seq, mate, fvsend.at[far]).wait_send()

    @pl.when(core == 0)
    def _():
        k_copy(k_ref, seq, mate, fksend.at[chip]).wait_send()
        v_copy(seq, mate, fvsend.at[chip]).wait_send()

    @pl.loop(chip + 1, chips)
    def _(far):
        k_copy(k_ref, seq, mate, ksend.at[far]).wait_send()
        v_copy(seq, mate, vsend.at[far]).wait_send()

    own_page.wait()

    @pl.loop(1, count)
    def _(step):
        other = lax.rem(block + step, count)
        page_copy(step).wait_send()
        pltpu.make_async_remote_copy(
            src_ref=pages.at[other], dst_ref=arrived_ref.at[other],
            send_sem=psend.at[other], recv_sem=precv.at[other],
            device_id=(section, seq, tensor), device_id_type=MESH,
        ).wait_recv()


def decode_kernel(
    count, gang,
    table_ref, length_ref,
    sq_ref, sk_ref, sv_ref, poolk_ref, poolv_ref, arrived_ref, early_ref, total_ref,
    q_ref, karch_ref, varch_ref,
    final_ref, out_ref,
    kpages, vpages, q_all, new_part, sems,
    q_slow, k_slow, v_slow, o_slow,
):
    copies = [pltpu.make_async_copy(early_ref, final_ref, sems.at[0])]
    pieces = 4
    size = POOL // pieces
    loads = []
    for i in range(pieces):
        span = pl.ds(i * size, size)
        loads.append(pltpu.make_async_copy(poolk_ref.at[span], kpages.at[span], sems.at[1 + 2 * i]))
        loads.append(pltpu.make_async_copy(poolv_ref.at[span], vpages.at[span], sems.at[2 + 2 * i]))
    place = pl.ds(POOL, count)
    loads.append(pltpu.make_async_copy(arrived_ref.at[:, pl.ds(0, PAGE)], kpages.at[place], sems.at[9]))
    loads.append(pltpu.make_async_copy(arrived_ref.at[:, pl.ds(PAGE, PAGE)], vpages.at[place], sems.at[10]))
    for copy in loads + copies:
        copy.start()

    for r in range(REQS):
        wide = sq_ref[r].astype(jnp.float32)
        q_all[r] = jnp.concatenate(
            [wide[:, h * HD:(h + 1) * HD] for h in range(GROUP)], axis=0
        ).astype(jnp.bfloat16)
    new_k = jnp.concatenate([sk_ref[r].astype(jnp.float32) for r in range(REQS)], 0).astype(jnp.bfloat16)
    new_v = jnp.concatenate([sv_ref[r].astype(jnp.float32) for r in range(REQS)], 0).astype(jnp.bfloat16)
    new_scores = dot_nt(q_all[...].reshape(REQS * ROWS, HD), new_k)
    shape = (REQS * ROWS, REQS * STEPS)
    row = lax.broadcasted_iota(jnp.int32, shape, 0)
    column = lax.broadcasted_iota(jnp.int32, shape, 1)
    fits = (column // STEPS == row // ROWS) & (column % STEPS <= row % STEPS)
    new_part[...] = jnp.where(fits, new_scores, LOW).reshape(REQS, ROWS, REQS * STEPS)

    for copy in loads:
        copy.wait()

    position = lax.broadcasted_iota(jnp.int32, (ROWS, CTX), 1)
    cut = 8

    @pl.loop(0, REQS // gang)
    def _(turn):
        scores, extras = [], []
        for g in range(gang):
            r = turn * gang + g
            q = q_all[r]
            parts = []
            for b in range(MAXPG // cut):
                keys = jnp.concatenate([kpages[table_ref[r, b * cut + i]] for i in range(cut)], axis=0)
                parts.append(dot_nt(q, keys))
            scores.append(jnp.where(position < length_ref[r], jnp.concatenate(parts, axis=1), LOW))
            extras.append(new_part[r])
        for g in range(gang):
            r = turn * gang + g
            top = jnp.maximum(
                jnp.max(scores[g], axis=1, keepdims=True), jnp.max(extras[g], axis=1, keepdims=True)
            )
            weights = jnp.exp2((scores[g] - top) * SCALE)
            extra = jnp.exp2((extras[g] - top) * SCALE)
            total = jnp.sum(weights, axis=1, keepdims=True) + jnp.sum(extra, axis=1, keepdims=True)
            weights = weights.astype(jnp.bfloat16)
            summed = dot_nn(extra.astype(jnp.bfloat16), new_v)
            for b in range(MAXPG // cut):
                values = jnp.concatenate([vpages[table_ref[r, b * cut + i]] for i in range(cut)], axis=0)
                summed += dot_nn(weights[:, b * cut * PAGE:(b + 1) * cut * PAGE], values)
            result = summed / total
            out_ref[r] = jnp.concatenate(
                [result[h * STEPS:(h + 1) * STEPS] for h in range(GROUP)], axis=1
            ).astype(jnp.bfloat16)

    for copy in copies:
        copy.wait()

    fine = jnp.min(jnp.where(total_ref[...] < LIMIT, 1.0, 0.0)) > 0.5

    @pl.when(jnp.logical_not(fine))
    def _():
        seq = lax.axis_index("seq")
        load = pltpu.make_async_copy(q_ref, q_slow, sems.at[0])
        load.start()
        load.wait()
        key_at = lax.broadcasted_iota(jnp.int32, (TOK, TOK), 0)
        query_at = lax.broadcasted_iota(jnp.int32, (TOK, TOK), 1)
        for head in range(GROUP):
            q = q_slow[0, :, head * HD:(head + 1) * HD]

            def advance(held, state):
                top, state_acc = state
                loads = (
                    pltpu.make_async_copy(karch_ref.at[held], k_slow, sems.at[1]),
                    pltpu.make_async_copy(varch_ref.at[held], v_slow, sems.at[2]),
                )
                for copy in loads:
                    copy.start()
                for copy in loads:
                    copy.wait()
                valid = key_at + held * TOK <= query_at + seq * TOK
                s = jnp.where(valid, dot_nt(k_slow[...].reshape(TOK, HD), q), LOW)
                fresh = jnp.maximum(top, jnp.max(s, axis=0, keepdims=True))
                w = jnp.exp2((s - fresh) * SCALE).astype(jnp.bfloat16)
                return fresh, state_acc * jnp.exp2((top - fresh) * SCALE) + dot_nn(v_slow[...], w)

            start = (jnp.full((1, TOK), LOW, jnp.float32), jnp.zeros((VROWS, TOK), jnp.float32))
            _, state = lax.fori_loop(0, seq + 1, lambda i, s: advance(seq - i, s), start)
            o_slow[0, :, head * HD:(head + 1) * HD] = (state[:HD] / state[HD:HD + 1]).astype(jnp.bfloat16).T
        store = pltpu.make_async_copy(o_slow, final_ref, sems.at[0])
        store.start()
        store.wait()


def on_device(
    prompt_query, prompt_keys, prompt_values, page_owner, pool_keys, pool_values,
    step_query, step_keys, step_values, page_table, context_len,
):
    sections = lax.axis_size("section")
    width = lax.axis_size("seq")
    count = sections * width
    chips = width // 2
    bf16, f32 = jnp.bfloat16, jnp.float32
    vmem = pl.BlockSpec(memory_space=pltpu.VMEM)
    smem = pl.BlockSpec(memory_space=pltpu.SMEM)
    hbm = pl.BlockSpec(memory_space=pl.ANY)
    pages = TOK // PAGE
    dma = pltpu.SemaphoreType.DMA
    early, totals, karch, varch, arrived = pl.pallas_call(
        functools.partial(prefill_kernel, chips, sections),
        out_shape=(
            jax.ShapeDtypeStruct((1, TOK, GROUP * HD), bf16),
            jax.ShapeDtypeStruct((GROUP, TOK), f32),
            jax.ShapeDtypeStruct((width, pages, PAGE, HD), bf16),
            jax.ShapeDtypeStruct((width, VROWS, TOK), bf16),
            jax.ShapeDtypeStruct((count, 2 * PAGE, HD), bf16),
        ),
        in_specs=[vmem, vmem, vmem, smem],
        out_specs=(vmem, vmem, hbm, hbm, hbm),
        scratch_shapes=[
            pltpu.VMEM((width, pages, PAGE, HD), bf16),
            pltpu.VMEM((width, VROWS, TOK), bf16),
            pltpu.VMEM((GROUP, VROWS, TOK), f32),
            pltpu.VMEM((GROUP, 1, TOK), f32),
            pltpu.VMEM((count, 2 * PAGE, HD), bf16),
            dma((chips,)), dma((chips,)), dma((width,)), dma((width,)),
            dma((chips,)), dma((chips,)), dma((count,)), dma((count,)),
            dma((1 + 2 * width,)),
        ],
        compiler_params=pltpu.CompilerParams(
            collective_id=0, has_side_effects=True, vmem_limit_bytes=32 * 2**20
        ),
        name="prefill",
    )(
        prompt_query,
        prompt_keys.reshape(pages, PAGE, HD),
        prompt_values.reshape(pages, PAGE, HD),
        page_owner,
    )
    return pl.pallas_call(
        functools.partial(decode_kernel, count, 4),
        out_shape=(
            jax.ShapeDtypeStruct((1, TOK, GROUP * HD), bf16),
            jax.ShapeDtypeStruct((REQS, STEPS, GROUP * HD), bf16),
        ),
        in_specs=[smem, smem, vmem, vmem, vmem, hbm, hbm, hbm, hbm, vmem, hbm, hbm, hbm],
        out_specs=(hbm, vmem),
        scratch_shapes=[
            pltpu.VMEM((POOL + count, PAGE, HD), bf16),
            pltpu.VMEM((POOL + count, PAGE, HD), bf16),
            pltpu.VMEM((REQS, ROWS, HD), bf16),
            pltpu.VMEM((REQS, ROWS, REQS * STEPS), f32),
            dma((11,)),
            pltpu.VMEM((1, TOK, GROUP * HD), bf16),
            pltpu.VMEM((pages, PAGE, HD), bf16),
            pltpu.VMEM((VROWS, TOK), bf16),
            pltpu.VMEM((1, TOK, GROUP * HD), bf16),
        ],
        compiler_params=pltpu.CompilerParams(vmem_limit_bytes=32 * 2**20),
        name="decode",
    )(
        page_table, context_len, step_query, step_keys, step_values, pool_keys, pool_values,
        arrived, early, totals, prompt_query, karch, varch,
    )


def solution(mesh):
    in_specs = (
        P("section", "seq", "tensor"),
        P("section", "seq", "tensor"),
        P("section", "seq", "tensor"),
        P("section", "seq"),
        P(("section", "seq"), None, "tensor"),
        P(("section", "seq"), None, "tensor"),
        P(("section", "seq"), None, "tensor"),
        P(("section", "seq"), None, "tensor"),
        P(("section", "seq"), None, "tensor"),
        P(("section", "seq"), None),
        P(("section", "seq")),
    )
    out_specs = (P("section", "seq", "tensor"), P(("section", "seq"), None, "tensor"))
    return jax.shard_map(
        on_device, mesh=mesh, in_specs=in_specs, out_specs=out_specs, check_vma=False
    )
```

```python
import functools
import math

import jax
import jax.numpy as jnp
from jax import lax
from jax.experimental import pallas as pl
from jax.experimental.pallas import tpu as pltpu
from jax.sharding import PartitionSpec as P

MESH = pl.DeviceIdType.MESH
HD = 128
PAGE = 32
MAXPG = 64
STEPS = 4
GROUP = 8
TOK = 512
VROWS = 144
POOL = 256
REQS = 16
CTX = MAXPG * PAGE
ROWS = STEPS * GROUP
SCALE = math.log2(math.e) / math.sqrt(HD)
LIMIT = 2.0**100
LOW = -1e30
NT = (((1,), (1,)), ((), ()))


def dot_nt(a, b):
    return lax.dot_general(a, b, NT, preferred_element_type=jnp.float32)


def dot_nn(a, b):
    return jnp.dot(a, b, preferred_element_type=jnp.float32)


def prefill_kernel(
    chips, sections,
    q_hbm, k_hbm, v_hbm, owner_hbm, poolk_hbm, poolv_hbm,
    out_ref, total_ref, kall, vall, pages,
    q_ref, k_ref, v_ref, owner_ref, acc, shift, outgoing,
    ksend, vsend, krecv, vrecv, fksend, fvsend, psend, precv, asem,
):
    section = lax.axis_index("section")
    seq = lax.axis_index("seq")
    tensor = lax.axis_index("tensor")
    width = 2 * chips
    count = sections * width
    chip, core = seq // 2, seq % 2
    mate = chip * 2 + (1 - core)
    block = section * width + seq

    load_k = pltpu.make_async_copy(k_hbm, k_ref, asem.at[0])
    load_v = pltpu.make_async_copy(v_hbm, v_ref, asem.at[1])
    load_owner = pltpu.make_async_copy(owner_hbm, owner_ref, asem.at[2])
    load_q = pltpu.make_async_copy(q_hbm, q_ref, asem.at[3])
    for copy in (load_k, load_v, load_owner, load_q):
        copy.start()

    barrier = pltpu.get_barrier_semaphore()

    @pl.loop(1, count)
    def _(step):
        other = lax.rem(block + step, count)
        pl.semaphore_signal(
            barrier, inc=1,
            device_id=(other // width, lax.rem(other, width), tensor), device_id_type=MESH,
        )

    load_pool = [
        pltpu.make_async_copy(poolk_hbm, pages.at[pl.ds(0, POOL), pl.ds(0, PAGE)], asem.at[4]),
        pltpu.make_async_copy(poolv_hbm, pages.at[pl.ds(0, POOL), pl.ds(PAGE, PAGE)], asem.at[5]),
    ]
    for index in range(width):
        vall[index, HD:, :] = jnp.ones((VROWS - HD, TOK), jnp.bfloat16)
    load_v.wait()
    vall[seq, :HD, :] = v_ref[...].reshape(TOK, HD).T
    load_k.wait()
    kall[seq] = k_ref[...]
    load_owner.wait()

    def page_copy(step):
        other = lax.rem(block + step, count)
        return pltpu.make_async_remote_copy(
            src_ref=outgoing.at[other], dst_ref=pages.at[POOL + block],
            send_sem=psend.at[other], recv_sem=precv.at[block],
            device_id=(other // width, lax.rem(other, width), tensor), device_id_type=MESH,
        )

    def fill_page(target):
        place = jnp.int32(0)
        for page in range(TOK // PAGE):
            place = jnp.where(owner_ref[0, page] == target, page, place)
        outgoing[target, :PAGE, :] = k_ref[place]
        outgoing[target, PAGE:, :] = v_ref[place]

    @pl.loop(0, count)
    def _(target):
        fill_page(target)

    pl.semaphore_wait(barrier, count - 1)

    def k_copy(held, target, ssem):
        return pltpu.make_async_remote_copy(
            src_ref=kall.at[held], dst_ref=kall.at[held], send_sem=ssem, recv_sem=krecv.at[held],
            device_id=(section, target, tensor), device_id_type=MESH,
        )

    def v_copy(held, target, ssem):
        return pltpu.make_async_remote_copy(
            src_ref=vall.at[held, pl.ds(0, HD)], dst_ref=vall.at[held, pl.ds(0, HD)],
            send_sem=ssem, recv_sem=vrecv.at[held],
            device_id=(section, target, tensor), device_id_type=MESH,
        )

    def start_block(held, target, slot):
        k_copy(held, target, ksend.at[slot]).start()
        v_copy(held, target, vsend.at[slot]).start()

    def sent_block(slot):
        k_copy(seq, mate, ksend.at[slot]).wait_send()
        v_copy(seq, mate, vsend.at[slot]).wait_send()

    def got_block(held):
        k_copy(held, mate, ksend.at[0]).wait_recv()
        v_copy(held, mate, vsend.at[0]).wait_recv()

    def pass_block(held, slot):
        k_copy(held, mate, fksend.at[slot]).start()
        v_copy(held, mate, fvsend.at[slot]).start()

    def passed_block(slot):
        k_copy(seq, mate, fksend.at[slot]).wait_send()
        v_copy(seq, mate, fvsend.at[slot]).wait_send()

    up = chip < chips - 1
    down = (chip == 0) | ((chip == 1) & (core == 1))

    @pl.when(core == 0)
    def _():
        pass_block(seq, chip)

    @pl.when(up)
    def _():
        start_block(seq, (chip + 1) * 2 + core, 0)

    @pl.when(down)
    def _():
        start_block(seq, lax.rem(chip + chips - 1, chips) * 2 + core, 1)

    for copy in load_pool:
        copy.start()
    load_q.wait()

    ones = jnp.ones((8, HD), jnp.bfloat16)
    half = TOK // 2
    own_k = k_ref[...].reshape(TOK, HD)
    k_low, k_high = own_k[:half], own_k[half:]
    key_at = lax.broadcasted_iota(jnp.int32, (half, TOK), 0)
    query_at = lax.broadcasted_iota(jnp.int32, (half, TOK), 1)
    low_valid = key_at <= query_at
    high_valid = low_valid[:, :half]

    def query(head):
        return q_ref[0, :, head * HD:(head + 1) * HD]

    shifts = []
    for head in range(GROUP):
        product = (query(head).astype(jnp.float32) * own_k.astype(jnp.float32)).astype(jnp.bfloat16)
        shifts.append(dot_nt(ones, product)[:1])
    for head in range(GROUP):
        shift[head] = shifts[head]

    def own_scores(head):
        q = query(head)
        return dot_nt(k_low, q), dot_nt(k_high, q[half:])

    scores = own_scores(0)
    for head in range(GROUP):
        following = own_scores(head + 1) if head + 1 < GROUP else None
        base = shift[head]
        low = jnp.where(low_valid, jnp.exp2((scores[0] - base) * SCALE), 0.0)
        high = jnp.where(high_valid, jnp.exp2((scores[1] - base[:, half:]) * SCALE), 0.0)
        first = dot_nn(vall[seq, :, :half], low.astype(jnp.bfloat16))
        second = dot_nn(vall[seq, :, half:], high.astype(jnp.bfloat16))
        acc[head, :, :half] = first[:, :half]
        acc[head, :, half:] = first[:, half:] + second
        scores = following

    def attend(held):
        keys = kall[held].reshape(TOK, HD)
        values = vall[held]
        scores = dot_nt(keys, query(0))
        for head in range(GROUP):
            following = dot_nt(keys, query(head + 1)) if head + 1 < GROUP else None
            weights = jnp.exp2((scores - shift[head]) * SCALE).astype(jnp.bfloat16)
            acc[head] += dot_nn(values, weights)
            scores = following

    def start_pages():
        @pl.when(up)
        def _():
            sent_block(0)

        @pl.when(down)
        def _():
            sent_block(1)

        @pl.loop(1, count)
        def _(step):
            page_copy(step).start()

    relays = ((chip == 0) & (core == 1)) | ((chip == 1) & (core == 0))
    relays = relays | ((chip == 2) & (core == 0)) | ((chip == 3) & (core == 1))

    def near_blocks():
        first = (chip - 1) * 2 + core
        got_block(first)

        @pl.when((core == 0) & (chip < 3))
        def _():
            start_block(first, (chip + 1) * 2 + core, 2)

        pass_block(first, chip - 1)

        @pl.when(chip == 3)
        def _():
            got_block(core)

            @pl.when(core == 1)
            def _():
                start_block(core, 2 * 2 + core, 2)

            pass_block(core, 0)

        start_pages()

    @pl.loop(0, core + 2 * chip)
    def _(step):
        turn = step - core

        @pl.when(turn == 0)
        def _():
            near_blocks()

        last = (chip == 3) & (turn >= 4)
        edge = (chip == 3) & (turn < 4)
        far = jnp.where(edge, 2 - 2 * (turn % 2), jnp.where(last, 1, chip - 1 - turn // 2))
        straight = jnp.where(edge, turn < 2, turn % 2 == 0)
        held = jnp.where(turn < 0, mate, far * 2 + jnp.where(straight, core, 1 - core))
        beyond = (turn >= 0) & straight & ((last) | ((chip == 2) & (turn >= 2)))

        @pl.when(jnp.logical_not((turn >= 0) & straight) | beyond)
        def _():
            got_block(held)

        @pl.when(beyond)
        def _():
            pass_block(held, far)

        attend(held)

    @pl.when(chip == 0)
    def _():
        start_pages()

        @pl.when(core == 1)
        def _():
            got_block(2 + core)
            start_block(2 + core, 3 * 2 + core, 2)

    for head in range(GROUP):
        state = acc[head]
        total = state[HD:HD + 1]
        total_ref[head:head + 1, :] = total
        out_ref[0, :, head * HD:(head + 1) * HD] = (state[:HD] / total).astype(jnp.bfloat16).T

    @pl.loop(0, chip)
    def _(far):
        passed_block(far)

    @pl.when(core == 0)
    def _():
        passed_block(chip)

    @pl.when(relays)
    def _():
        sent_block(2)

    for copy in load_pool:
        copy.wait()
    pages[POOL + block] = outgoing[block]

    @pl.loop(1, count)
    def _(step):
        other = lax.rem(block + step, count)
        page_copy(step).wait_send()
        pltpu.make_async_remote_copy(
            src_ref=outgoing.at[other], dst_ref=pages.at[POOL + other],
            send_sem=psend.at[other], recv_sem=precv.at[other],
            device_id=(section, mate, tensor), device_id_type=MESH,
        ).wait_recv()


def decode_kernel(
    gang,
    table_hbm, length_hbm, sq_hbm, sk_hbm, sv_hbm, pages, early_ref, total_ref,
    q_ref, karch_ref, varch_ref,
    final_ref, out_ref,
    table_ref, length_ref, sq_ref, sk_ref, sv_ref, q_all, new_part, sems,
    q_slow, k_slow, v_slow, o_slow,
):
    sources = (early_ref, table_hbm, length_hbm, sq_hbm, sk_hbm, sv_hbm)
    targets = (final_ref, table_ref, length_ref, sq_ref, sk_ref, sv_ref)
    loads = [pltpu.make_async_copy(x, y, sems.at[i]) for i, (x, y) in enumerate(zip(sources, targets))]
    for copy in loads[1:]:
        copy.start()
    loads[0].start()
    for copy in loads[1:]:
        copy.wait()

    for r in range(REQS):
        wide = sq_ref[r].astype(jnp.float32)
        q_all[r] = jnp.concatenate(
            [wide[:, h * HD:(h + 1) * HD] for h in range(GROUP)], axis=0
        ).astype(jnp.bfloat16)
    new_k = jnp.concatenate([sk_ref[r].astype(jnp.float32) for r in range(REQS)], 0).astype(jnp.bfloat16)
    new_v = jnp.concatenate([sv_ref[r].astype(jnp.float32) for r in range(REQS)], 0).astype(jnp.bfloat16)
    new_scores = dot_nt(q_all[...].reshape(REQS * ROWS, HD), new_k)
    shape = (REQS * ROWS, REQS * STEPS)
    row = lax.broadcasted_iota(jnp.int32, shape, 0)
    column = lax.broadcasted_iota(jnp.int32, shape, 1)
    fits = (column // STEPS == row // ROWS) & (column % STEPS <= row % STEPS)
    new_part[...] = jnp.where(fits, new_scores, LOW).reshape(REQS, ROWS, REQS * STEPS)

    position = lax.broadcasted_iota(jnp.int32, (ROWS, CTX), 1)
    cut = 8

    @pl.loop(0, REQS // gang)
    def _(turn):
        scores, extras = [], []
        for g in range(gang):
            r = turn * gang + g
            q = q_all[r]
            parts = []
            for b in range(MAXPG // cut):
                keys = jnp.concatenate([pages[table_ref[r, b * cut + i], :PAGE] for i in range(cut)], axis=0)
                parts.append(dot_nt(q, keys))
            scores.append(jnp.where(position < length_ref[r], jnp.concatenate(parts, axis=1), LOW))
            extras.append(new_part[r])
        for g in range(gang):
            r = turn * gang + g
            top = jnp.maximum(
                jnp.max(scores[g], axis=1, keepdims=True), jnp.max(extras[g], axis=1, keepdims=True)
            )
            weights = jnp.exp2((scores[g] - top) * SCALE)
            extra = jnp.exp2((extras[g] - top) * SCALE)
            total = jnp.sum(weights, axis=1, keepdims=True) + jnp.sum(extra, axis=1, keepdims=True)
            weights = weights.astype(jnp.bfloat16)
            summed = dot_nn(extra.astype(jnp.bfloat16), new_v)
            for b in range(MAXPG // cut):
                values = jnp.concatenate([pages[table_ref[r, b * cut + i], PAGE:] for i in range(cut)], axis=0)
                summed += dot_nn(weights[:, b * cut * PAGE:(b + 1) * cut * PAGE], values)
            result = summed / total
            out_ref[r] = jnp.concatenate(
                [result[h * STEPS:(h + 1) * STEPS] for h in range(GROUP)], axis=1
            ).astype(jnp.bfloat16)

    loads[0].wait()

    fine = jnp.min(jnp.where(total_ref[...] < LIMIT, 1.0, 0.0)) > 0.5

    @pl.when(jnp.logical_not(fine))
    def _():
        seq = lax.axis_index("seq")
        load = pltpu.make_async_copy(q_ref, q_slow, sems.at[0])
        load.start()
        load.wait()
        key_at = lax.broadcasted_iota(jnp.int32, (TOK, TOK), 0)
        query_at = lax.broadcasted_iota(jnp.int32, (TOK, TOK), 1)
        for head in range(GROUP):
            q = q_slow[0, :, head * HD:(head + 1) * HD]

            def advance(held, state):
                top, state_acc = state
                loads = (
                    pltpu.make_async_copy(karch_ref.at[held], k_slow, sems.at[1]),
                    pltpu.make_async_copy(varch_ref.at[held], v_slow, sems.at[2]),
                )
                for copy in loads:
                    copy.start()
                for copy in loads:
                    copy.wait()
                valid = key_at + held * TOK <= query_at + seq * TOK
                s = jnp.where(valid, dot_nt(k_slow[...].reshape(TOK, HD), q), LOW)
                fresh = jnp.maximum(top, jnp.max(s, axis=0, keepdims=True))
                w = jnp.exp2((s - fresh) * SCALE).astype(jnp.bfloat16)
                return fresh, state_acc * jnp.exp2((top - fresh) * SCALE) + dot_nn(v_slow[...], w)

            start = (jnp.full((1, TOK), LOW, jnp.float32), jnp.zeros((VROWS, TOK), jnp.float32))
            _, state = lax.fori_loop(0, seq + 1, lambda i, s: advance(seq - i, s), start)
            o_slow[0, :, head * HD:(head + 1) * HD] = (state[:HD] / state[HD:HD + 1]).astype(jnp.bfloat16).T
        store = pltpu.make_async_copy(o_slow, final_ref, sems.at[0])
        store.start()
        store.wait()


def in_hbm(array):
    return pltpu.with_memory_space_constraint(array, pltpu.HBM)


def on_device(
    prompt_query, prompt_keys, prompt_values, page_owner, pool_keys, pool_values,
    step_query, step_keys, step_values, page_table, context_len,
):
    sections = lax.axis_size("section")
    width = lax.axis_size("seq")
    count = sections * width
    chips = width // 2
    bf16, f32 = jnp.bfloat16, jnp.float32
    vmem = pl.BlockSpec(memory_space=pltpu.VMEM)
    hbm = pl.BlockSpec(memory_space=pltpu.HBM)
    anywhere = pl.BlockSpec(memory_space=pl.ANY)
    pages = TOK // PAGE
    dma = pltpu.SemaphoreType.DMA
    early, totals, karch, varch, held_pages = pl.pallas_call(
        functools.partial(prefill_kernel, chips, sections),
        out_shape=(
            jax.ShapeDtypeStruct((1, TOK, GROUP * HD), bf16),
            jax.ShapeDtypeStruct((GROUP, TOK), f32),
            jax.ShapeDtypeStruct((width, pages, PAGE, HD), bf16),
            jax.ShapeDtypeStruct((width, VROWS, TOK), bf16),
            jax.ShapeDtypeStruct((POOL + count, 2 * PAGE, HD), bf16),
        ),
        in_specs=[hbm] * 6,
        out_specs=(vmem,) * 5,
        scratch_shapes=[
            pltpu.VMEM((1, TOK, GROUP * HD), bf16),
            pltpu.VMEM((pages, PAGE, HD), bf16),
            pltpu.VMEM((pages, PAGE, HD), bf16),
            pltpu.SMEM((1, pages), jnp.int32),
            pltpu.VMEM((GROUP, VROWS, TOK), f32),
            pltpu.VMEM((GROUP, 1, TOK), f32),
            pltpu.VMEM((count, 2 * PAGE, HD), bf16),
            dma((3,)), dma((3,)), dma((width,)), dma((width,)),
            dma((chips,)), dma((chips,)), dma((count,)), dma((count,)),
            dma((6,)),
        ],
        compiler_params=pltpu.CompilerParams(
            collective_id=0, has_side_effects=True, vmem_limit_bytes=32 * 2**20
        ),
        name="prefill",
    )(
        in_hbm(prompt_query),
        in_hbm(prompt_keys.reshape(pages, PAGE, HD)),
        in_hbm(prompt_values.reshape(pages, PAGE, HD)),
        in_hbm(page_owner),
        in_hbm(pool_keys),
        in_hbm(pool_values),
    )
    return pl.pallas_call(
        functools.partial(decode_kernel, 4),
        out_shape=(
            jax.ShapeDtypeStruct((1, TOK, GROUP * HD), bf16),
            jax.ShapeDtypeStruct((REQS, STEPS, GROUP * HD), bf16),
        ),
        in_specs=[hbm] * 5 + [vmem, anywhere, vmem, hbm, anywhere, anywhere],
        out_specs=(hbm, vmem),
        scratch_shapes=[
            pltpu.SMEM((REQS, MAXPG), jnp.int32),
            pltpu.SMEM((REQS,), jnp.int32),
            pltpu.VMEM((REQS, STEPS, GROUP * HD), bf16),
            pltpu.VMEM((REQS, STEPS, HD), bf16),
            pltpu.VMEM((REQS, STEPS, HD), bf16),
            pltpu.VMEM((REQS, ROWS, HD), bf16),
            pltpu.VMEM((REQS, ROWS, REQS * STEPS), f32),
            dma((6,)),
            pltpu.VMEM((1, TOK, GROUP * HD), bf16),
            pltpu.VMEM((pages, PAGE, HD), bf16),
            pltpu.VMEM((VROWS, TOK), bf16),
            pltpu.VMEM((1, TOK, GROUP * HD), bf16),
        ],
        compiler_params=pltpu.CompilerParams(vmem_limit_bytes=32 * 2**20),
        name="decode",
    )(
        in_hbm(page_table), in_hbm(context_len), in_hbm(step_query), in_hbm(step_keys), in_hbm(step_values),
        held_pages, early, totals, in_hbm(prompt_query), karch, varch,
    )


def solution(mesh):
    in_specs = (
        P("section", "seq", "tensor"),
        P("section", "seq", "tensor"),
        P("section", "seq", "tensor"),
        P("section", "seq"),
        P(("section", "seq"), None, "tensor"),
        P(("section", "seq"), None, "tensor"),
        P(("section", "seq"), None, "tensor"),
        P(("section", "seq"), None, "tensor"),
        P(("section", "seq"), None, "tensor"),
        P(("section", "seq"), None),
        P(("section", "seq")),
    )
    out_specs = (P("section", "seq", "tensor"), P(("section", "seq"), None, "tensor"))
    return jax.shard_map(
        on_device, mesh=mesh, in_specs=in_specs, out_specs=out_specs, check_vma=False
    )
```

```python
import functools
import math

import jax
import jax.numpy as jnp
from jax import lax
from jax.experimental import pallas as pl
from jax.experimental.pallas import tpu as pltpu
from jax.sharding import PartitionSpec as P

MESH = pl.DeviceIdType.MESH
HD = 128
PAGE = 32
MAXPG = 64
STEPS = 4
GROUP = 8
TOK = 512
VROWS = 144
HALF = TOK // 2
SLABS = HALF // PAGE
POOL = 256
REQS = 16
CTX = MAXPG * PAGE
ROWS = STEPS * GROUP
SCALE = math.log2(math.e) / math.sqrt(HD)
LIMIT = 2.0**100
LOW = -1e30
NT = (((1,), (1,)), ((), ()))


def dot_nt(a, b):
    return lax.dot_general(a, b, NT, preferred_element_type=jnp.float32)


def dot_nn(a, b):
    return jnp.dot(a, b, preferred_element_type=jnp.float32)


def prefill_kernel(
    chips, sections,
    q_hbm, k_hbm, v_hbm, owner_hbm, poolk_hbm, poolv_hbm, sq_hbm, sk_hbm, sv_hbm,
    out_ref, total_ref, kall, vall, pages, q_all, new_part, new_v,
    sq_ref, sk_ref, sv_ref, q_ref, own, prev, following, beyond, passed,
    table0, table1, table2, table3, owner0, owner1, owner2, owner3,
    acc, shift, outgoing,
    nsend, rsend, drecv, msend, mrecv, tsend, trecv, psend, precv, asem,
):
    section = lax.axis_index("section")
    seq = lax.axis_index("seq")
    tensor = lax.axis_index("tensor")
    width = 2 * chips
    chip, core = seq // 2, seq % 2
    mate = chip * 2 + (1 - core)
    block = section * width + seq
    above = lax.rem(chip + 1, chips)
    below = lax.rem(chip + chips - 1, chips)
    across = lax.rem(chip + 2, chips)
    origin = (chip, below, above, across)
    held = tuple(c * 2 + core for c in origin)
    direct = (own, prev, following, beyond)
    tables = (table0, table1, table2, table3)
    owners = (owner0, owner1, owner2, owner3)

    def place(row, target):
        return (row, target, tensor)

    loads = [
        pltpu.make_async_copy(k_hbm, own.at[0], asem.at[0]),
        pltpu.make_async_copy(v_hbm, own.at[1], asem.at[1]),
        pltpu.make_async_copy(owner_hbm, table0, asem.at[2]),
        pltpu.make_async_copy(owner_hbm, owner0, asem.at[3]),
        pltpu.make_async_copy(sq_hbm, sq_ref, asem.at[10]),
        pltpu.make_async_copy(sk_hbm, sk_ref, asem.at[11]),
        pltpu.make_async_copy(sv_hbm, sv_ref, asem.at[12]),
        pltpu.make_async_copy(q_hbm, q_ref, asem.at[4]),
    ]
    load_pool = [
        pltpu.make_async_copy(poolk_hbm, pages.at[pl.ds(0, POOL), pl.ds(0, PAGE)], asem.at[5]),
        pltpu.make_async_copy(poolv_hbm, pages.at[pl.ds(0, POOL), pl.ds(PAGE, PAGE)], asem.at[6]),
    ]
    for copy in loads:
        copy.start()

    barrier = pltpu.get_barrier_semaphore()
    peers = [place(section, above * 2 + core), place(section, below * 2 + core), place(section, mate)]
    for offset in range(1, sections):
        for other in range(2):
            peers.append(place(lax.rem(section + offset, sections), chip * 2 + other))
    for peer in peers:
        pl.semaphore_signal(barrier, inc=1, device_id=peer, device_id_type=MESH)

    for index in range(2 * width):
        vall[index, HD:, :] = jnp.ones((VROWS - HD, HALF), jnp.bfloat16)
    for copy in loads[:7]:
        copy.wait()
    prepare(sq_ref, sk_ref, sv_ref, q_all, new_part, new_v)
    pl.semaphore_wait(barrier, len(peers))

    def part(ref, half):
        return ref.at[:, pl.ds(half * SLABS, SLABS)]

    def near_copy(up, half):
        return pltpu.make_async_remote_copy(
            src_ref=part(own, half), dst_ref=part(prev if up else following, half),
            send_sem=nsend.at[0 if up else 1, half], recv_sem=drecv.at[1 if up else 2, half],
            device_id=place(section, (above if up else below) * 2 + core), device_id_type=MESH,
        )

    def near_table(up):
        return pltpu.make_async_remote_copy(
            src_ref=table0, dst_ref=table1 if up else table2,
            send_sem=tsend.at[0 if up else 1], recv_sem=trecv.at[1 if up else 2],
            device_id=place(section, (above if up else below) * 2 + core), device_id_type=MESH,
        )

    def relay_copy(up, half):
        return pltpu.make_async_remote_copy(
            src_ref=part(prev if up else following, half), dst_ref=part(beyond, half),
            send_sem=rsend.at[half], recv_sem=drecv.at[3, half],
            device_id=place(section, (above if up else below) * 2 + core), device_id_type=MESH,
        )

    def relay_table(up):
        return pltpu.make_async_remote_copy(
            src_ref=table1 if up else table2, dst_ref=table3,
            send_sem=tsend.at[2], recv_sem=trecv.at[3],
            device_id=place(section, (above if up else below) * 2 + core), device_id_type=MESH,
        )

    def mate_copy(kind, half):
        return pltpu.make_async_remote_copy(
            src_ref=part(direct[kind], half), dst_ref=part(passed.at[kind], half),
            send_sem=msend.at[kind, half], recv_sem=mrecv.at[kind, half],
            device_id=place(section, mate), device_id_type=MESH,
        )

    def page_copy(kind, offset, other):
        row = lax.rem(section + offset, sections)
        return pltpu.make_async_remote_copy(
            src_ref=outgoing.at[kind, offset * 2 + other],
            dst_ref=pages.at[POOL + section * width + held[kind]],
            send_sem=psend.at[kind, offset * 2 + other],
            recv_sem=precv.at[section * width + held[kind]],
            device_id=place(row, chip * 2 + other), device_id_type=MESH,
        )

    def local_owners(kind):
        return pltpu.make_async_copy(tables[kind], owners[kind], asem.at[6 + kind])

    def send_pages(kind):
        for offset in range(sections):
            for other in range(2):
                row = lax.rem(section + offset, sections)
                taker = row * width + chip * 2 + other
                slot = jnp.int32(0)
                for page in range(TOK // PAGE):
                    slot = jnp.where(owners[kind][0, page] == taker, page, slot)
                outgoing[kind, offset * 2 + other, :PAGE, :] = direct[kind][0, slot]
                outgoing[kind, offset * 2 + other, PAGE:, :] = direct[kind][1, slot]
        for offset in range(1, sections):
            for other in range(2):
                page_copy(kind, offset, other).start()
        for other in range(2):
            @pl.when(core == other)
            def _():
                pages[POOL + section * width + held[kind]] = outgoing[kind, other]

            @pl.when(core != other)
            def _():
                page_copy(kind, 0, other).start()

    for half in range(2):
        near_copy(True, half).start()
        near_copy(False, half).start()
    near_table(True).start()
    near_table(False).start()

    @pl.when(core == 0)
    def _():
        mate_copy(0, 0).start()
        mate_copy(0, 1).start()

    for copy in load_pool:
        copy.start()

    def slab(half):
        return slice(half * SLABS, (half + 1) * SLABS)

    for half in range(2):
        kall[seq * 2 + half] = own[0, slab(half)]
        vall[seq * 2 + half, :HD, :] = own[1, slab(half)].reshape(HALF, HD).T
    loads[7].wait()

    ones = jnp.ones((8, HD), jnp.bfloat16)
    own_k = own[0].reshape(TOK, HD)
    k_low, k_high = own_k[:HALF], own_k[HALF:]
    key_at = lax.broadcasted_iota(jnp.int32, (HALF, TOK), 0)
    query_at = lax.broadcasted_iota(jnp.int32, (HALF, TOK), 1)
    low_valid = key_at <= query_at
    high_valid = low_valid[:, :HALF]

    def query(head):
        return q_ref[0, :, head * HD:(head + 1) * HD]

    shifts = []
    for head in range(GROUP):
        product = (query(head).astype(jnp.float32) * own_k.astype(jnp.float32)).astype(jnp.bfloat16)
        shifts.append(dot_nt(ones, product)[:1])
    for head in range(GROUP):
        shift[head] = shifts[head]

    def own_scores(head):
        q = query(head)
        return dot_nt(k_low, q), dot_nt(k_high, q[HALF:])

    scores = own_scores(0)
    for head in range(GROUP):
        upcoming = own_scores(head + 1) if head + 1 < GROUP else None
        base = shift[head]
        low = jnp.where(low_valid, jnp.exp2((scores[0] - base) * SCALE), 0.0)
        high = jnp.where(high_valid, jnp.exp2((scores[1] - base[:, HALF:]) * SCALE), 0.0)
        first = dot_nn(vall[seq * 2], low.astype(jnp.bfloat16))
        second = dot_nn(vall[seq * 2 + 1], high.astype(jnp.bfloat16))
        acc[head, :, :HALF] = first[:, :HALF]
        acc[head, :, HALF:] = first[:, HALF:] + second
        scores = upcoming

    def attend(first, second):
        keys = jnp.concatenate([kall[first].reshape(HALF, HD), kall[second].reshape(HALF, HD)], axis=0)
        values = jnp.concatenate([vall[first], vall[second]], axis=1)
        scores = dot_nt(keys, query(0))
        for head in range(GROUP):
            upcoming = dot_nt(keys, query(head + 1)) if head + 1 < GROUP else None
            weights = jnp.exp2((scores - shift[head]) * SCALE).astype(jnp.bfloat16)
            acc[head] += dot_nn(values, weights)
            scores = upcoming

    def take(kind, half):
        kall[held[kind] * 2 + half] = direct[kind][0, slab(half)]
        vall[held[kind] * 2 + half, :HD, :] = direct[kind][1, slab(half)].reshape(HALF, HD).T

    def arrive(kind, half):
        pltpu.make_async_remote_copy(
            src_ref=part(own, half), dst_ref=part(direct[kind], half),
            send_sem=rsend.at[half], recv_sem=drecv.at[kind, half],
            device_id=place(section, mate), device_id_type=MESH,
        ).wait_recv()
        if kind < 3:
            @pl.when(core == kind - 1)
            def _():
                relay_copy(kind == 1, half).start()

        @pl.when(origin[kind] < chip)
        def _():
            mate_copy(kind, half).start()
            take(kind, half)

    def forward_pages(kind):
        pltpu.make_async_remote_copy(
            src_ref=table0, dst_ref=tables[kind], send_sem=tsend.at[2], recv_sem=trecv.at[kind],
            device_id=place(section, mate), device_id_type=MESH,
        ).wait_recv()
        if kind < 3:
            @pl.when(core == kind - 1)
            def _():
                relay_table(kind == 1).start()
        local_owners(kind).start()
        local_owners(kind).wait()
        send_pages(kind)

    edge = chip == chips - 1
    second_turn = jnp.where(edge, 2, 0)
    far_turn = jnp.where(chip == 0, 1, chip)

    @pl.loop(0, core + jnp.maximum(2 * chip, 2))
    def _(step):
        turn = step - core

        @pl.when(turn == 0)
        def _():
            arrive(1, 0)
            arrive(2, 0)
            send_pages(0)

        @pl.when(turn == second_turn)
        def _():
            arrive(1, 1)
            arrive(2, 1)
            forward_pages(1)
            forward_pages(2)

        @pl.when(turn == far_turn)
        def _():
            arrive(3, 0)
            arrive(3, 1)
            forward_pages(3)

        both = edge & (turn >= 0) & (turn < 4)
        single = jnp.where(turn < 0, 0, jnp.where(turn < 2, 1, 3))
        single = jnp.where(edge & (turn >= 4), 3, single)
        kinds = (jnp.where(both, 1, single), jnp.where(both, 2, single))
        halves = (jnp.where(both, turn // 2, 0), jnp.where(both, turn // 2, 1))
        straight = (turn >= 0) & (turn % 2 == 0)
        wanted = (turn < 0) | (turn < 2 * chip)
        indices = []
        for kind, half in zip(kinds, halves):
            move = jnp.where(kind == 1, chips - 1, jnp.where(kind == 2, 1, jnp.where(kind == 3, 2, 0)))
            index = (lax.rem(chip + move, chips) * 2 + jnp.where(straight, core, 1 - core)) * 2 + half
            indices.append(index)

            @pl.when(wanted & jnp.logical_not(straight))
            def _():
                pltpu.make_async_remote_copy(
                    src_ref=part(own, 0), dst_ref=part(passed.at[kind], half),
                    send_sem=rsend.at[0], recv_sem=mrecv.at[kind, half],
                    device_id=place(section, mate), device_id_type=MESH,
                ).wait_recv()
                kall[index] = passed[kind, 0, pl.ds(half * SLABS, SLABS)]
                vall[index, :HD, :] = passed[kind, 1, pl.ds(half * SLABS, SLABS)].reshape(HALF, HD).T

        @pl.when(wanted)
        def _():
            attend(*indices)

    for head in range(GROUP):
        state = acc[head]
        total = state[HD:HD + 1]
        total_ref[head:head + 1, :] = total
        out_ref[0, :, head * HD:(head + 1) * HD] = (state[:HD] * (1.0 / total)).astype(jnp.bfloat16).T

    for up in (True, False):
        near_table(up).wait_send()
        for half in range(2):
            near_copy(up, half).wait_send()
    relay_table(True).wait_send()
    for half in range(2):
        relay_copy(True, half).wait_send()

        @pl.when(core == 0)
        def _():
            mate_copy(0, half).wait_send()

        for kind in (1, 2, 3):
            @pl.when(origin[kind] < chip)
            def _():
                mate_copy(kind, half).wait_send()

    for copy in load_pool:
        copy.wait()

    for kind in range(4):
        for offset in range(1, sections):
            for other in range(2):
                page_copy(kind, offset, other).wait_send()
        for other in range(2):
            @pl.when(core != other)
            def _():
                page_copy(kind, 0, other).wait_send()

    @pl.loop(0, sections)
    def _(row):
        @pl.loop(0, width)
        def _(far):
            @pl.when((row != section) | (far % 2 != core))
            def _():
                pltpu.make_async_remote_copy(
                    src_ref=outgoing.at[0, 0], dst_ref=pages.at[POOL + row * width + far],
                    send_sem=psend.at[0, 0], recv_sem=precv.at[row * width + far],
                    device_id=place(section, mate), device_id_type=MESH,
                ).wait_recv()


def prepare(sq_ref, sk_ref, sv_ref, q_all, new_part, new_v):
    for r in range(REQS):
        wide = sq_ref[r].astype(jnp.float32)
        q_all[r] = jnp.concatenate(
            [wide[:, h * HD:(h + 1) * HD] for h in range(GROUP)], axis=0
        ).astype(jnp.bfloat16)
    new_k = jnp.concatenate([sk_ref[r].astype(jnp.float32) for r in range(REQS)], 0).astype(jnp.bfloat16)
    new_v[...] = jnp.concatenate([sv_ref[r].astype(jnp.float32) for r in range(REQS)], 0).astype(jnp.bfloat16)
    new_scores = dot_nt(q_all[...].reshape(REQS * ROWS, HD), new_k)
    shape = (REQS * ROWS, REQS * STEPS)
    row = lax.broadcasted_iota(jnp.int32, shape, 0)
    column = lax.broadcasted_iota(jnp.int32, shape, 1)
    fits = (column // STEPS == row // ROWS) & (column % STEPS <= row % STEPS)
    new_part[...] = jnp.where(fits, new_scores, LOW).reshape(REQS, ROWS, REQS * STEPS)


def decode_kernel(
    gang,
    table_hbm, length_hbm, pages, q_all, new_part, new_v, early_ref, total_ref,
    q_ref, karch_ref, varch_ref,
    final_ref, out_ref,
    table_ref, length_ref, sems, q_slow, k_slow, v_slow, o_slow,
):
    loads = [
        pltpu.make_async_copy(early_ref, final_ref, sems.at[0]),
        pltpu.make_async_copy(table_hbm, table_ref, sems.at[1]),
        pltpu.make_async_copy(length_hbm, length_ref, sems.at[2]),
    ]
    for copy in loads[1:]:
        copy.start()
    loads[0].start()
    for copy in loads[1:]:
        copy.wait()

    position = lax.broadcasted_iota(jnp.int32, (ROWS, CTX), 1)
    cut = 8

    @pl.loop(0, REQS // gang)
    def _(turn):
        scores, extras = [], []
        for g in range(gang):
            r = turn * gang + g
            q = q_all[r]
            parts = []
            for b in range(MAXPG // cut):
                keys = jnp.concatenate([pages[table_ref[r, b * cut + i], :PAGE] for i in range(cut)], axis=0)
                parts.append(dot_nt(q, keys))
            scores.append(jnp.where(position < length_ref[r], jnp.concatenate(parts, axis=1), LOW))
            extras.append(new_part[r])
        for g in range(gang):
            r = turn * gang + g
            top = jnp.maximum(
                jnp.max(scores[g], axis=1, keepdims=True), jnp.max(extras[g], axis=1, keepdims=True)
            )
            weights = jnp.exp2((scores[g] - top) * SCALE)
            extra = jnp.exp2((extras[g] - top) * SCALE)
            total = jnp.sum(weights, axis=1, keepdims=True) + jnp.sum(extra, axis=1, keepdims=True)
            weights = weights.astype(jnp.bfloat16)
            summed = dot_nn(extra.astype(jnp.bfloat16), new_v[...])
            for b in range(MAXPG // cut):
                values = jnp.concatenate([pages[table_ref[r, b * cut + i], PAGE:] for i in range(cut)], axis=0)
                summed += dot_nn(weights[:, b * cut * PAGE:(b + 1) * cut * PAGE], values)
            result = summed / total
            out_ref[r] = jnp.concatenate(
                [result[h * STEPS:(h + 1) * STEPS] for h in range(GROUP)], axis=1
            ).astype(jnp.bfloat16)

    loads[0].wait()

    fine = jnp.min(jnp.where(total_ref[...] < LIMIT, 1.0, 0.0)) > 0.5

    @pl.when(jnp.logical_not(fine))
    def _():
        seq = lax.axis_index("seq")
        load = pltpu.make_async_copy(q_ref, q_slow, sems.at[0])
        load.start()
        load.wait()
        key_at = lax.broadcasted_iota(jnp.int32, (HALF, TOK), 0)
        query_at = lax.broadcasted_iota(jnp.int32, (HALF, TOK), 1)
        for head in range(GROUP):
            q = q_slow[0, :, head * HD:(head + 1) * HD]

            def advance(held, state):
                top, state_acc = state
                loads = (
                    pltpu.make_async_copy(karch_ref.at[held], k_slow, sems.at[1]),
                    pltpu.make_async_copy(varch_ref.at[held], v_slow, sems.at[2]),
                )
                for copy in loads:
                    copy.start()
                for copy in loads:
                    copy.wait()
                valid = key_at + held * HALF <= query_at + seq * TOK
                s = jnp.where(valid, dot_nt(k_slow[...].reshape(HALF, HD), q), LOW)
                fresh = jnp.maximum(top, jnp.max(s, axis=0, keepdims=True))
                w = jnp.exp2((s - fresh) * SCALE).astype(jnp.bfloat16)
                return fresh, state_acc * jnp.exp2((top - fresh) * SCALE) + dot_nn(v_slow[...], w)

            start = (jnp.full((1, TOK), LOW, jnp.float32), jnp.zeros((VROWS, TOK), jnp.float32))
            _, state = lax.fori_loop(0, 2 * seq + 2, advance, start)
            o_slow[0, :, head * HD:(head + 1) * HD] = (state[:HD] / state[HD:HD + 1]).astype(jnp.bfloat16).T
        store = pltpu.make_async_copy(o_slow, final_ref, sems.at[0])
        store.start()
        store.wait()


def in_hbm(array):
    return pltpu.with_memory_space_constraint(array, pltpu.HBM)


def on_device(
    prompt_query, prompt_keys, prompt_values, page_owner, pool_keys, pool_values,
    step_query, step_keys, step_values, page_table, context_len,
):
    sections = lax.axis_size("section")
    width = lax.axis_size("seq")
    count = sections * width
    chips = width // 2
    bf16, f32 = jnp.bfloat16, jnp.float32
    vmem = pl.BlockSpec(memory_space=pltpu.VMEM)
    hbm = pl.BlockSpec(memory_space=pltpu.HBM)
    anywhere = pl.BlockSpec(memory_space=pl.ANY)
    pages = TOK // PAGE
    dma = pltpu.SemaphoreType.DMA
    early, totals, karch, varch, held_pages, q_all, new_part, new_v = pl.pallas_call(
        functools.partial(prefill_kernel, chips, sections),
        out_shape=(
            jax.ShapeDtypeStruct((1, TOK, GROUP * HD), bf16),
            jax.ShapeDtypeStruct((GROUP, TOK), f32),
            jax.ShapeDtypeStruct((2 * width, SLABS, PAGE, HD), bf16),
            jax.ShapeDtypeStruct((2 * width, VROWS, HALF), bf16),
            jax.ShapeDtypeStruct((POOL + count, 2 * PAGE, HD), bf16),
            jax.ShapeDtypeStruct((REQS, ROWS, HD), bf16),
            jax.ShapeDtypeStruct((REQS, ROWS, REQS * STEPS), f32),
            jax.ShapeDtypeStruct((REQS * STEPS, HD), bf16),
        ),
        in_specs=[hbm] * 9,
        out_specs=(vmem,) * 8,
        scratch_shapes=[
            pltpu.VMEM((REQS, STEPS, GROUP * HD), bf16),
            pltpu.VMEM((REQS, STEPS, HD), bf16),
            pltpu.VMEM((REQS, STEPS, HD), bf16),
            pltpu.VMEM((1, TOK, GROUP * HD), bf16),
            *[pltpu.VMEM((2, pages, PAGE, HD), bf16)] * 4,
            pltpu.VMEM((4, 2, pages, PAGE, HD), bf16),
            *[pltpu.VMEM((1, pages), jnp.int32)] * 4,
            *[pltpu.SMEM((1, pages), jnp.int32)] * 4,
            pltpu.VMEM((GROUP, VROWS, TOK), f32),
            pltpu.VMEM((GROUP, 1, TOK), f32),
            pltpu.VMEM((4, 2 * sections, 2 * PAGE, HD), bf16),
            dma((2, 2)), dma((2,)), dma((4, 2)), dma((4, 2)), dma((4, 2)),
            dma((3,)), dma((4,)), dma((4, 2 * sections)), dma((count,)),
            dma((13,)),
        ],
        compiler_params=pltpu.CompilerParams(
            collective_id=0, has_side_effects=True, vmem_limit_bytes=32 * 2**20
        ),
        name="prefill",
    )(
        in_hbm(prompt_query),
        in_hbm(prompt_keys.reshape(pages, PAGE, HD)),
        in_hbm(prompt_values.reshape(pages, PAGE, HD)),
        in_hbm(page_owner),
        in_hbm(pool_keys),
        in_hbm(pool_values),
        in_hbm(step_query),
        in_hbm(step_keys),
        in_hbm(step_values),
    )
    return pl.pallas_call(
        functools.partial(decode_kernel, REQS),
        out_shape=(
            jax.ShapeDtypeStruct((1, TOK, GROUP * HD), bf16),
            jax.ShapeDtypeStruct((REQS, STEPS, GROUP * HD), bf16),
        ),
        in_specs=[hbm] * 2 + [vmem] * 4 + [anywhere, vmem, hbm, anywhere, anywhere],
        out_specs=(hbm, vmem),
        scratch_shapes=[
            pltpu.SMEM((REQS, MAXPG), jnp.int32),
            pltpu.SMEM((REQS,), jnp.int32),
            dma((3,)),
            pltpu.VMEM((1, TOK, GROUP * HD), bf16),
            pltpu.VMEM((SLABS, PAGE, HD), bf16),
            pltpu.VMEM((VROWS, HALF), bf16),
            pltpu.VMEM((1, TOK, GROUP * HD), bf16),
        ],
        compiler_params=pltpu.CompilerParams(vmem_limit_bytes=32 * 2**20),
        name="decode",
    )(
        in_hbm(page_table), in_hbm(context_len), held_pages, q_all, new_part, new_v,
        early, totals, in_hbm(prompt_query), karch, varch,
    )


def solution(mesh):
    in_specs = (
        P("section", "seq", "tensor"),
        P("section", "seq", "tensor"),
        P("section", "seq", "tensor"),
        P("section", "seq"),
        P(("section", "seq"), None, "tensor"),
        P(("section", "seq"), None, "tensor"),
        P(("section", "seq"), None, "tensor"),
        P(("section", "seq"), None, "tensor"),
        P(("section", "seq"), None, "tensor"),
        P(("section", "seq"), None),
        P(("section", "seq")),
    )
    out_specs = (P("section", "seq", "tensor"), P(("section", "seq"), None, "tensor"))
    return jax.shard_map(
        on_device, mesh=mesh, in_specs=in_specs, out_specs=out_specs, check_vma=False
    )
```

```python
import functools
import math

import jax
import jax.numpy as jnp
from jax import lax
from jax.experimental import pallas as pl
from jax.experimental.pallas import tpu as pltpu
from jax.sharding import PartitionSpec as P

MESH = pl.DeviceIdType.MESH
HD = 128
PAGE = 32
MAXPG = 64
STEPS = 4
GROUP = 8
TOK = 512
VROWS = 144
HALF = TOK // 2
SLABS = HALF // PAGE
POOL = 256
REQS = 16
CTX = MAXPG * PAGE
ROWS = STEPS * GROUP
SCALE = math.log2(math.e) / math.sqrt(HD)
LIMIT = 2.0**100
LOW = -1e30
NT = (((1,), (1,)), ((), ()))


def dot_nt(a, b):
    return lax.dot_general(a, b, NT, preferred_element_type=jnp.float32)


def dot_nn(a, b):
    return jnp.dot(a, b, preferred_element_type=jnp.float32)


def prefill_kernel(
    chips, sections,
    q_hbm, k_hbm, v_hbm, owner_hbm, poolk_hbm, poolv_hbm, sq_hbm, sk_hbm, sv_hbm,
    out_ref, total_ref, kall, vall, pages, q_all, new_part, new_v,
    sq_ref, sk_ref, sv_ref, q_ref, own, prev, following, beyond, passed,
    table0, table1, table2, table3, owner0, owner1, owner2, owner3,
    acc, shift, outgoing,
    nsend, rsend, drecv, msend, mrecv, tsend, trecv, psend, precv, asem,
):
    section = lax.axis_index("section")
    seq = lax.axis_index("seq")
    tensor = lax.axis_index("tensor")
    width = 2 * chips
    chip, core = seq // 2, seq % 2
    mate = chip * 2 + (1 - core)
    block = section * width + seq
    above = lax.rem(chip + 1, chips)
    below = lax.rem(chip + chips - 1, chips)
    across = lax.rem(chip + 2, chips)
    origin = (chip, below, above, across)
    held = tuple(c * 2 + core for c in origin)
    direct = (own, prev, following, beyond)
    tables = (table0, table1, table2, table3)
    owners = (owner0, owner1, owner2, owner3)

    def place(row, target):
        return (row, target, tensor)

    loads = [
        pltpu.make_async_copy(k_hbm, own.at[0], asem.at[0]),
        pltpu.make_async_copy(v_hbm, own.at[1], asem.at[1]),
        pltpu.make_async_copy(owner_hbm, table0, asem.at[2]),
        pltpu.make_async_copy(owner_hbm, owner0, asem.at[3]),
        pltpu.make_async_copy(sq_hbm, sq_ref, asem.at[10]),
        pltpu.make_async_copy(sk_hbm, sk_ref, asem.at[11]),
        pltpu.make_async_copy(sv_hbm, sv_ref, asem.at[12]),
        pltpu.make_async_copy(q_hbm, q_ref, asem.at[4]),
    ]
    load_pool = [
        pltpu.make_async_copy(poolk_hbm, pages.at[pl.ds(0, POOL), pl.ds(0, PAGE)], asem.at[5]),
        pltpu.make_async_copy(poolv_hbm, pages.at[pl.ds(0, POOL), pl.ds(PAGE, PAGE)], asem.at[6]),
    ]
    for copy in loads:
        copy.start()

    barrier = pltpu.get_barrier_semaphore()
    peers = [place(section, above * 2 + core), place(section, below * 2 + core), place(section, mate)]
    for offset in range(1, sections):
        for other in range(2):
            peers.append(place(lax.rem(section + offset, sections), chip * 2 + other))
    for peer in peers:
        pl.semaphore_signal(barrier, inc=1, device_id=peer, device_id_type=MESH)

    for index in range(2 * width):
        vall[index, HD:, :] = jnp.ones((VROWS - HD, HALF), jnp.bfloat16)
    for copy in loads[:7]:
        copy.wait()
    prepare(sq_ref, sk_ref, sv_ref, q_all, new_part, new_v)
    pl.semaphore_wait(barrier, len(peers))

    def part(ref, half):
        return ref.at[:, pl.ds(half * SLABS, SLABS)]

    def near_copy(up, half):
        return pltpu.make_async_remote_copy(
            src_ref=part(own, half), dst_ref=part(prev if up else following, half),
            send_sem=nsend.at[0 if up else 1, half], recv_sem=drecv.at[1 if up else 2, half],
            device_id=place(section, (above if up else below) * 2 + core), device_id_type=MESH,
        )

    def near_table(up):
        return pltpu.make_async_remote_copy(
            src_ref=table0, dst_ref=table1 if up else table2,
            send_sem=tsend.at[0 if up else 1], recv_sem=trecv.at[1 if up else 2],
            device_id=place(section, (above if up else below) * 2 + core), device_id_type=MESH,
        )

    def relay_copy(up, half):
        return pltpu.make_async_remote_copy(
            src_ref=part(prev if up else following, half), dst_ref=part(beyond, half),
            send_sem=rsend.at[half], recv_sem=drecv.at[3, half],
            device_id=place(section, (above if up else below) * 2 + core), device_id_type=MESH,
        )

    def relay_table(up):
        return pltpu.make_async_remote_copy(
            src_ref=table1 if up else table2, dst_ref=table3,
            send_sem=tsend.at[2], recv_sem=trecv.at[3],
            device_id=place(section, (above if up else below) * 2 + core), device_id_type=MESH,
        )

    def mate_copy(kind, half):
        return pltpu.make_async_remote_copy(
            src_ref=part(direct[kind], half), dst_ref=part(passed.at[kind], half),
            send_sem=msend.at[kind, half], recv_sem=mrecv.at[kind, half],
            device_id=place(section, mate), device_id_type=MESH,
        )

    def page_copy(kind, offset, other):
        row = lax.rem(section + offset, sections)
        return pltpu.make_async_remote_copy(
            src_ref=outgoing.at[kind, offset * 2 + other],
            dst_ref=pages.at[POOL + section * width + held[kind]],
            send_sem=psend.at[kind, offset * 2 + other],
            recv_sem=precv.at[section * width + held[kind]],
            device_id=place(row, chip * 2 + other), device_id_type=MESH,
        )

    def local_owners(kind):
        return pltpu.make_async_copy(tables[kind], owners[kind], asem.at[6 + kind])

    def send_pages(kind):
        for offset in range(sections):
            for other in range(2):
                row = lax.rem(section + offset, sections)
                taker = row * width + chip * 2 + other
                slot = jnp.int32(0)
                for page in range(TOK // PAGE):
                    slot = jnp.where(owners[kind][0, page] == taker, page, slot)
                outgoing[kind, offset * 2 + other, :PAGE, :] = direct[kind][0, slot]
                outgoing[kind, offset * 2 + other, PAGE:, :] = direct[kind][1, slot]
        for offset in range(1, sections):
            for other in range(2):
                page_copy(kind, offset, other).start()
        for other in range(2):
            @pl.when(core == other)
            def _():
                pages[POOL + section * width + held[kind]] = outgoing[kind, other]

            @pl.when(core != other)
            def _():
                page_copy(kind, 0, other).start()

    for half in range(2):
        near_copy(True, half).start()
        near_copy(False, half).start()
    near_table(True).start()
    near_table(False).start()

    @pl.when(core == 0)
    def _():
        mate_copy(0, 0).start()
        mate_copy(0, 1).start()

    for copy in load_pool:
        copy.start()

    def slab(half):
        return slice(half * SLABS, (half + 1) * SLABS)

    for half in range(2):
        kall[seq * 2 + half] = own[0, slab(half)]
        vall[seq * 2 + half, :HD, :] = own[1, slab(half)].reshape(HALF, HD).T
    loads[7].wait()

    ones = jnp.ones((8, HD), jnp.bfloat16)
    own_k = own[0].reshape(TOK, HD)
    k_low, k_high = own_k[:HALF], own_k[HALF:]
    key_at = lax.broadcasted_iota(jnp.int32, (HALF, TOK), 0)
    query_at = lax.broadcasted_iota(jnp.int32, (HALF, TOK), 1)
    low_valid = key_at <= query_at
    high_valid = low_valid[:, :HALF]

    def query(head):
        return q_ref[0, :, head * HD:(head + 1) * HD]

    shifts = []
    for head in range(GROUP):
        product = (query(head).astype(jnp.float32) * own_k.astype(jnp.float32)).astype(jnp.bfloat16)
        shifts.append(dot_nt(ones, product)[:1])
    for head in range(GROUP):
        shift[head] = shifts[head]

    def own_scores(head):
        q = query(head)
        return dot_nt(k_low, q), dot_nt(k_high, q[HALF:])

    scores = own_scores(0)
    for head in range(GROUP):
        upcoming = own_scores(head + 1) if head + 1 < GROUP else None
        base = shift[head]
        low = jnp.where(low_valid, jnp.exp2((scores[0] - base) * SCALE), 0.0)
        high = jnp.where(high_valid, jnp.exp2((scores[1] - base[:, HALF:]) * SCALE), 0.0)
        first = dot_nn(vall[seq * 2], low.astype(jnp.bfloat16))
        second = dot_nn(vall[seq * 2 + 1], high.astype(jnp.bfloat16))
        acc[head, :, :HALF] = first[:, :HALF]
        acc[head, :, HALF:] = first[:, HALF:] + second
        scores = upcoming

    def attend(*taken):
        keys = jnp.concatenate([kall[index].reshape(HALF, HD) for index in taken], axis=0)
        values = jnp.concatenate([vall[index] for index in taken], axis=1)
        scores = dot_nt(keys, query(0))
        for head in range(GROUP):
            upcoming = dot_nt(keys, query(head + 1)) if head + 1 < GROUP else None
            weights = jnp.exp2((scores - shift[head]) * SCALE).astype(jnp.bfloat16)
            acc[head] += dot_nn(values, weights)
            scores = upcoming

    def take(kind, half):
        kall[held[kind] * 2 + half] = direct[kind][0, slab(half)]
        vall[held[kind] * 2 + half, :HD, :] = direct[kind][1, slab(half)].reshape(HALF, HD).T

    def arrive(kind, half):
        pltpu.make_async_remote_copy(
            src_ref=part(own, half), dst_ref=part(direct[kind], half),
            send_sem=rsend.at[half], recv_sem=drecv.at[kind, half],
            device_id=place(section, mate), device_id_type=MESH,
        ).wait_recv()
        if kind < 3:
            @pl.when(core == kind - 1)
            def _():
                relay_copy(kind == 1, half).start()

        @pl.when(origin[kind] < chip)
        def _():
            mate_copy(kind, half).start()
            take(kind, half)

    def forward_pages(kind):
        pltpu.make_async_remote_copy(
            src_ref=table0, dst_ref=tables[kind], send_sem=tsend.at[2], recv_sem=trecv.at[kind],
            device_id=place(section, mate), device_id_type=MESH,
        ).wait_recv()
        if kind < 3:
            @pl.when(core == kind - 1)
            def _():
                relay_table(kind == 1).start()
        local_owners(kind).start()
        local_owners(kind).wait()
        send_pages(kind)

    edge = chip == chips - 1
    turns = jnp.maximum(2 * chip, 2)
    visits = turns // 2

    def ready(turn, active):
        both = edge & (turn >= 0) & (turn < 4)
        single = jnp.where(turn < 0, 0, jnp.where(turn < 2, 1, 3))
        single = jnp.where(edge & (turn >= 4), 3, single)
        kinds = (jnp.where(both, 1, single), jnp.where(both, 2, single))
        halves = (jnp.where(both, turn // 2, 0), jnp.where(both, turn // 2, 1))
        straight = (turn >= 0) & (turn % 2 == 0)
        indices = []
        for kind, half in zip(kinds, halves):
            move = jnp.where(kind == 1, chips - 1, jnp.where(kind == 2, 1, jnp.where(kind == 3, 2, 0)))
            index = (lax.rem(chip + move, chips) * 2 + jnp.where(straight, core, 1 - core)) * 2 + half
            indices.append(index)

            @pl.when(active & jnp.logical_not(straight))
            def _():
                pltpu.make_async_remote_copy(
                    src_ref=part(own, 0), dst_ref=part(passed.at[kind], half),
                    send_sem=rsend.at[0], recv_sem=mrecv.at[kind, half],
                    device_id=place(section, mate), device_id_type=MESH,
                ).wait_recv()
                kall[index] = passed[kind, 0, pl.ds(half * SLABS, SLABS)]
                vall[index, :HD, :] = passed[kind, 1, pl.ds(half * SLABS, SLABS)].reshape(HALF, HD).T

        return indices

    @pl.loop(0, core + 1 + visits)
    def _(step):
        visit = step - core

        @pl.when(visit == 0)
        def _():
            send_pages(0)
            arrive(1, 0)
            arrive(2, 0)

        @pl.when(visit == jnp.where(edge, 1, 0))
        def _():
            arrive(1, 1)
            arrive(2, 1)
            forward_pages(1)
            forward_pages(2)

        @pl.when(visit == jnp.where(edge, 2, 1))
        def _():
            arrive(3, 0)
            arrive(3, 1)
            forward_pages(3)

        paired = (visit >= 1) & (visit < visits)
        turn = jnp.where(visit <= 0, visit, jnp.where(paired, 2 * visit - 1, turns - 1))
        wanted = (turn < 0) | (turn < 2 * chip)
        indices = ready(turn, wanted)

        @pl.when(wanted & jnp.logical_not(paired))
        def _():
            attend(*indices)

        @pl.when(paired)
        def _():
            after = turn + 1
            both = edge & (after < 4)
            kinds = (jnp.where(both, 1, 3), jnp.where(both, 2, 3))
            halves = (jnp.where(both, 1, 0), 1)
            more = []
            for kind, half in zip(kinds, halves):
                move = jnp.where(kind == 1, chips - 1, jnp.where(kind == 2, 1, 2))
                more.append((lax.rem(chip + move, chips) * 2 + core) * 2 + half)
            attend(*indices, *more)

    for head in range(GROUP):
        state = acc[head]
        total = state[HD:HD + 1]
        total_ref[head:head + 1, :] = total
        out_ref[0, :, head * HD:(head + 1) * HD] = (state[:HD] * (1.0 / total)).astype(jnp.bfloat16).T

    for up in (True, False):
        near_table(up).wait_send()
        for half in range(2):
            near_copy(up, half).wait_send()
    relay_table(True).wait_send()
    for half in range(2):
        relay_copy(True, half).wait_send()

        @pl.when(core == 0)
        def _():
            mate_copy(0, half).wait_send()

        for kind in (1, 2, 3):
            @pl.when(origin[kind] < chip)
            def _():
                mate_copy(kind, half).wait_send()

    for copy in load_pool:
        copy.wait()

    for kind in range(4):
        for offset in range(1, sections):
            for other in range(2):
                page_copy(kind, offset, other).wait_send()
        for other in range(2):
            @pl.when(core != other)
            def _():
                page_copy(kind, 0, other).wait_send()

    @pl.loop(0, sections)
    def _(row):
        @pl.loop(0, width)
        def _(far):
            @pl.when((row != section) | (far % 2 != core))
            def _():
                pltpu.make_async_remote_copy(
                    src_ref=outgoing.at[0, 0], dst_ref=pages.at[POOL + row * width + far],
                    send_sem=psend.at[0, 0], recv_sem=precv.at[row * width + far],
                    device_id=place(section, mate), device_id_type=MESH,
                ).wait_recv()


def prepare(sq_ref, sk_ref, sv_ref, q_all, new_part, new_v):
    for r in range(REQS):
        wide = sq_ref[r].astype(jnp.float32)
        q_all[r] = jnp.concatenate(
            [wide[:, h * HD:(h + 1) * HD] for h in range(GROUP)], axis=0
        ).astype(jnp.bfloat16)
    new_k = jnp.concatenate([sk_ref[r].astype(jnp.float32) for r in range(REQS)], 0).astype(jnp.bfloat16)
    new_v[...] = jnp.concatenate([sv_ref[r].astype(jnp.float32) for r in range(REQS)], 0).astype(jnp.bfloat16)
    new_scores = dot_nt(q_all[...].reshape(REQS * ROWS, HD), new_k)
    shape = (REQS * ROWS, REQS * STEPS)
    row = lax.broadcasted_iota(jnp.int32, shape, 0)
    column = lax.broadcasted_iota(jnp.int32, shape, 1)
    fits = (column // STEPS == row // ROWS) & (column % STEPS <= row % STEPS)
    new_part[...] = jnp.where(fits, new_scores, LOW).reshape(REQS, ROWS, REQS * STEPS)


def decode_kernel(
    table_hbm, length_hbm, pages, q_all, new_part, new_v, early_ref, total_ref,
    q_ref, karch_ref, varch_ref,
    final_ref, out_ref,
    table_ref, length_ref, sems, q_slow, k_slow, v_slow, o_slow,
):
    loads = [
        pltpu.make_async_copy(early_ref, final_ref, sems.at[0]),
        pltpu.make_async_copy(table_hbm, table_ref, sems.at[1]),
        pltpu.make_async_copy(length_hbm, length_ref, sems.at[2]),
    ]
    for copy in loads[1:]:
        copy.start()
    loads[0].start()
    for copy in loads[1:]:
        copy.wait()

    position = lax.broadcasted_iota(jnp.int32, (ROWS, CTX), 1)
    cut = 8

    def gather(r, b, low):
        return jnp.concatenate(
            [pages[table_ref[r, b * cut + i], low:low + PAGE] for i in range(cut)], axis=0
        )

    def score(r):
        q = q_all[r]
        parts = [dot_nt(q, gather(r, b, 0)) for b in range(MAXPG // cut)]
        return jnp.concatenate(parts, axis=1)

    def weigh(r, scores):
        scores = jnp.where(position < length_ref[r], scores, LOW)
        extra = new_part[r]
        top = jnp.maximum(jnp.max(scores, axis=1, keepdims=True), jnp.max(extra, axis=1, keepdims=True))
        weights = jnp.exp2((scores - top) * SCALE)
        extra = jnp.exp2((extra - top) * SCALE)
        total = jnp.sum(weights, axis=1, keepdims=True) + jnp.sum(extra, axis=1, keepdims=True)
        return weights.astype(jnp.bfloat16), extra.astype(jnp.bfloat16), total

    def combine(r, weights, extra, total):
        summed = dot_nn(extra, new_v[...])
        for b in range(MAXPG // cut):
            summed += dot_nn(weights[:, b * cut * PAGE:(b + 1) * cut * PAGE], gather(r, b, PAGE))
        result = summed / total
        out_ref[r] = jnp.concatenate(
            [result[h * STEPS:(h + 1) * STEPS] for h in range(GROUP)], axis=1
        ).astype(jnp.bfloat16)

    ahead = score(0)
    waiting = None
    for r in range(REQS):
        upcoming = score(r + 1) if r + 1 < REQS else None
        weighed = weigh(r, ahead)
        if waiting is not None:
            combine(r - 1, *waiting)
        waiting, ahead = weighed, upcoming
    combine(REQS - 1, *waiting)

    loads[0].wait()

    fine = jnp.min(jnp.where(total_ref[...] < LIMIT, 1.0, 0.0)) > 0.5

    @pl.when(jnp.logical_not(fine))
    def _():
        seq = lax.axis_index("seq")
        load = pltpu.make_async_copy(q_ref, q_slow, sems.at[0])
        load.start()
        load.wait()
        key_at = lax.broadcasted_iota(jnp.int32, (HALF, TOK), 0)
        query_at = lax.broadcasted_iota(jnp.int32, (HALF, TOK), 1)
        for head in range(GROUP):
            q = q_slow[0, :, head * HD:(head + 1) * HD]

            def advance(held, state):
                top, state_acc = state
                loads = (
                    pltpu.make_async_copy(karch_ref.at[held], k_slow, sems.at[1]),
                    pltpu.make_async_copy(varch_ref.at[held], v_slow, sems.at[2]),
                )
                for copy in loads:
                    copy.start()
                for copy in loads:
                    copy.wait()
                valid = key_at + held * HALF <= query_at + seq * TOK
                s = jnp.where(valid, dot_nt(k_slow[...].reshape(HALF, HD), q), LOW)
                fresh = jnp.maximum(top, jnp.max(s, axis=0, keepdims=True))
                w = jnp.exp2((s - fresh) * SCALE).astype(jnp.bfloat16)
                return fresh, state_acc * jnp.exp2((top - fresh) * SCALE) + dot_nn(v_slow[...], w)

            start = (jnp.full((1, TOK), LOW, jnp.float32), jnp.zeros((VROWS, TOK), jnp.float32))
            _, state = lax.fori_loop(0, 2 * seq + 2, advance, start)
            o_slow[0, :, head * HD:(head + 1) * HD] = (state[:HD] / state[HD:HD + 1]).astype(jnp.bfloat16).T
        store = pltpu.make_async_copy(o_slow, final_ref, sems.at[0])
        store.start()
        store.wait()


def in_hbm(array):
    return pltpu.with_memory_space_constraint(array, pltpu.HBM)


def on_device(
    prompt_query, prompt_keys, prompt_values, page_owner, pool_keys, pool_values,
    step_query, step_keys, step_values, page_table, context_len,
):
    sections = lax.axis_size("section")
    width = lax.axis_size("seq")
    count = sections * width
    chips = width // 2
    bf16, f32 = jnp.bfloat16, jnp.float32
    vmem = pl.BlockSpec(memory_space=pltpu.VMEM)
    hbm = pl.BlockSpec(memory_space=pltpu.HBM)
    anywhere = pl.BlockSpec(memory_space=pl.ANY)
    pages = TOK // PAGE
    dma = pltpu.SemaphoreType.DMA
    early, totals, karch, varch, held_pages, q_all, new_part, new_v = pl.pallas_call(
        functools.partial(prefill_kernel, chips, sections),
        out_shape=(
            jax.ShapeDtypeStruct((1, TOK, GROUP * HD), bf16),
            jax.ShapeDtypeStruct((GROUP, TOK), f32),
            jax.ShapeDtypeStruct((2 * width, SLABS, PAGE, HD), bf16),
            jax.ShapeDtypeStruct((2 * width, VROWS, HALF), bf16),
            jax.ShapeDtypeStruct((POOL + count, 2 * PAGE, HD), bf16),
            jax.ShapeDtypeStruct((REQS, ROWS, HD), bf16),
            jax.ShapeDtypeStruct((REQS, ROWS, REQS * STEPS), f32),
            jax.ShapeDtypeStruct((REQS * STEPS, HD), bf16),
        ),
        in_specs=[hbm] * 9,
        out_specs=(vmem,) * 8,
        scratch_shapes=[
            pltpu.VMEM((REQS, STEPS, GROUP * HD), bf16),
            pltpu.VMEM((REQS, STEPS, HD), bf16),
            pltpu.VMEM((REQS, STEPS, HD), bf16),
            pltpu.VMEM((1, TOK, GROUP * HD), bf16),
            *[pltpu.VMEM((2, pages, PAGE, HD), bf16)] * 4,
            pltpu.VMEM((4, 2, pages, PAGE, HD), bf16),
            *[pltpu.VMEM((1, pages), jnp.int32)] * 4,
            *[pltpu.SMEM((1, pages), jnp.int32)] * 4,
            pltpu.VMEM((GROUP, VROWS, TOK), f32),
            pltpu.VMEM((GROUP, 1, TOK), f32),
            pltpu.VMEM((4, 2 * sections, 2 * PAGE, HD), bf16),
            dma((2, 2)), dma((2,)), dma((4, 2)), dma((4, 2)), dma((4, 2)),
            dma((3,)), dma((4,)), dma((4, 2 * sections)), dma((count,)),
            dma((13,)),
        ],
        compiler_params=pltpu.CompilerParams(
            collective_id=0, has_side_effects=True, vmem_limit_bytes=32 * 2**20
        ),
        name="prefill",
    )(
        in_hbm(prompt_query),
        in_hbm(prompt_keys.reshape(pages, PAGE, HD)),
        in_hbm(prompt_values.reshape(pages, PAGE, HD)),
        in_hbm(page_owner),
        in_hbm(pool_keys),
        in_hbm(pool_values),
        in_hbm(step_query),
        in_hbm(step_keys),
        in_hbm(step_values),
    )
    return pl.pallas_call(
        decode_kernel,
        out_shape=(
            jax.ShapeDtypeStruct((1, TOK, GROUP * HD), bf16),
            jax.ShapeDtypeStruct((REQS, STEPS, GROUP * HD), bf16),
        ),
        in_specs=[hbm] * 2 + [vmem] * 4 + [anywhere, vmem, hbm, anywhere, anywhere],
        out_specs=(hbm, vmem),
        scratch_shapes=[
            pltpu.SMEM((REQS, MAXPG), jnp.int32),
            pltpu.SMEM((REQS,), jnp.int32),
            dma((3,)),
            pltpu.VMEM((1, TOK, GROUP * HD), bf16),
            pltpu.VMEM((SLABS, PAGE, HD), bf16),
            pltpu.VMEM((VROWS, HALF), bf16),
            pltpu.VMEM((1, TOK, GROUP * HD), bf16),
        ],
        compiler_params=pltpu.CompilerParams(vmem_limit_bytes=32 * 2**20),
        name="decode",
    )(
        in_hbm(page_table), in_hbm(context_len), held_pages, q_all, new_part, new_v,
        early, totals, in_hbm(prompt_query), karch, varch,
    )


def solution(mesh):
    in_specs = (
        P("section", "seq", "tensor"),
        P("section", "seq", "tensor"),
        P("section", "seq", "tensor"),
        P("section", "seq"),
        P(("section", "seq"), None, "tensor"),
        P(("section", "seq"), None, "tensor"),
        P(("section", "seq"), None, "tensor"),
        P(("section", "seq"), None, "tensor"),
        P(("section", "seq"), None, "tensor"),
        P(("section", "seq"), None),
        P(("section", "seq")),
    )
    out_specs = (P("section", "seq", "tensor"), P(("section", "seq"), None, "tensor"))
    return jax.shard_map(
        on_device, mesh=mesh, in_specs=in_specs, out_specs=out_specs, check_vma=False
    )
```

```python
import functools
import math

import jax
import jax.numpy as jnp
from jax import lax
from jax.experimental import pallas as pl
from jax.experimental.pallas import tpu as pltpu
from jax.sharding import PartitionSpec as P

MESH = pl.DeviceIdType.MESH
HD = 128
PAGE = 32
MAXPG = 64
STEPS = 4
GROUP = 8
TOK = 512
VROWS = 144
HALF = TOK // 2
SLABS = HALF // PAGE
POOL = 256
REQS = 16
CTX = MAXPG * PAGE
ROWS = STEPS * GROUP
SCALE = math.log2(math.e) / math.sqrt(HD)
LIMIT = 2.0**100
LOW = -1e30
NT = (((1,), (1,)), ((), ()))


def dot_nt(a, b):
    return lax.dot_general(a, b, NT, preferred_element_type=jnp.float32)


def dot_nn(a, b):
    return jnp.dot(a, b, preferred_element_type=jnp.float32)


def prefill_kernel(
    chips, sections,
    q_hbm, k_hbm, v_hbm, owner_hbm, poolk_hbm, poolv_hbm, sq_hbm, sk_hbm, sv_hbm,
    out_ref, total_ref, kall, vall, pages, q_all, new_part, new_v,
    sq_ref, sk_ref, sv_ref, q_ref, own, prev, following, beyond, passed,
    table0, table1, table2, table3, owner0, owner1, owner2, owner3,
    acc, shift, outgoing,
    nsend, rsend, drecv, msend, mrecv, tsend, trecv, psend, precv, asem,
):
    section = lax.axis_index("section")
    seq = lax.axis_index("seq")
    tensor = lax.axis_index("tensor")
    width = 2 * chips
    chip, core = seq // 2, seq % 2
    mate = chip * 2 + (1 - core)
    block = section * width + seq
    above = lax.rem(chip + 1, chips)
    below = lax.rem(chip + chips - 1, chips)
    across = lax.rem(chip + 2, chips)
    origin = (chip, below, above, across)
    held = tuple(c * 2 + core for c in origin)
    direct = (own, prev, following, beyond)
    tables = (table0, table1, table2, table3)
    owners = (owner0, owner1, owner2, owner3)

    def place(row, target):
        return (row, target, tensor)

    loads = [
        pltpu.make_async_copy(k_hbm, own.at[0], asem.at[0]),
        pltpu.make_async_copy(v_hbm, own.at[1], asem.at[1]),
        pltpu.make_async_copy(owner_hbm, table0, asem.at[2]),
        pltpu.make_async_copy(owner_hbm, owner0, asem.at[3]),
        pltpu.make_async_copy(sq_hbm, sq_ref, asem.at[10]),
        pltpu.make_async_copy(sk_hbm, sk_ref, asem.at[11]),
        pltpu.make_async_copy(sv_hbm, sv_ref, asem.at[12]),
        pltpu.make_async_copy(q_hbm, q_ref, asem.at[4]),
    ]
    load_pool = [
        pltpu.make_async_copy(poolk_hbm, pages.at[pl.ds(0, POOL), pl.ds(0, PAGE)], asem.at[5]),
        pltpu.make_async_copy(poolv_hbm, pages.at[pl.ds(0, POOL), pl.ds(PAGE, PAGE)], asem.at[6]),
    ]
    for copy in loads:
        copy.start()

    barrier = pltpu.get_barrier_semaphore()
    peers = [place(section, above * 2 + core), place(section, below * 2 + core), place(section, mate)]
    for offset in range(1, sections):
        for other in range(2):
            peers.append(place(lax.rem(section + offset, sections), chip * 2 + other))
    for peer in peers:
        pl.semaphore_signal(barrier, inc=1, device_id=peer, device_id_type=MESH)

    for index in range(2 * width):
        vall[index, HD:, :] = jnp.ones((VROWS - HD, HALF), jnp.bfloat16)
    for copy in loads[:7]:
        copy.wait()
    prepare(sq_ref, sk_ref, sv_ref, q_all, new_part, new_v)
    pl.semaphore_wait(barrier, len(peers))

    def part(ref, half):
        return ref.at[:, pl.ds(half * SLABS, SLABS)]

    def near_copy(up, half):
        return pltpu.make_async_remote_copy(
            src_ref=part(own, half), dst_ref=part(prev if up else following, half),
            send_sem=nsend.at[0 if up else 1, half], recv_sem=drecv.at[1 if up else 2, half],
            device_id=place(section, (above if up else below) * 2 + core), device_id_type=MESH,
        )

    def near_table(up):
        return pltpu.make_async_remote_copy(
            src_ref=table0, dst_ref=table1 if up else table2,
            send_sem=tsend.at[0 if up else 1], recv_sem=trecv.at[1 if up else 2],
            device_id=place(section, (above if up else below) * 2 + core), device_id_type=MESH,
        )

    def relay_copy(up, half):
        return pltpu.make_async_remote_copy(
            src_ref=part(prev if up else following, half), dst_ref=part(beyond, half),
            send_sem=rsend.at[half], recv_sem=drecv.at[3, half],
            device_id=place(section, (above if up else below) * 2 + core), device_id_type=MESH,
        )

    def relay_table(up):
        return pltpu.make_async_remote_copy(
            src_ref=table1 if up else table2, dst_ref=table3,
            send_sem=tsend.at[2], recv_sem=trecv.at[3],
            device_id=place(section, (above if up else below) * 2 + core), device_id_type=MESH,
        )

    def mate_copy(kind, half):
        return pltpu.make_async_remote_copy(
            src_ref=part(direct[kind], half), dst_ref=part(passed.at[kind], half),
            send_sem=msend.at[kind, half], recv_sem=mrecv.at[kind, half],
            device_id=place(section, mate), device_id_type=MESH,
        )

    def page_copy(kind, offset, other):
        row = lax.rem(section + offset, sections)
        return pltpu.make_async_remote_copy(
            src_ref=outgoing.at[kind, offset * 2 + other],
            dst_ref=pages.at[POOL + section * width + held[kind]],
            send_sem=psend.at[kind, offset * 2 + other],
            recv_sem=precv.at[section * width + held[kind]],
            device_id=place(row, chip * 2 + other), device_id_type=MESH,
        )

    def local_owners(kind):
        return pltpu.make_async_copy(tables[kind], owners[kind], asem.at[6 + kind])

    def send_pages(kind):
        for offset in range(sections):
            for other in range(2):
                row = lax.rem(section + offset, sections)
                taker = row * width + chip * 2 + other
                slot = jnp.int32(0)
                for page in range(TOK // PAGE):
                    slot = jnp.where(owners[kind][0, page] == taker, page, slot)
                outgoing[kind, offset * 2 + other, :PAGE, :] = direct[kind][0, slot]
                outgoing[kind, offset * 2 + other, PAGE:, :] = direct[kind][1, slot]
        for offset in range(1, sections):
            for other in range(2):
                page_copy(kind, offset, other).start()
        for other in range(2):
            @pl.when(core == other)
            def _():
                pages[POOL + section * width + held[kind]] = outgoing[kind, other]

            @pl.when(core != other)
            def _():
                page_copy(kind, 0, other).start()

    near_table(True).start()
    near_table(False).start()
    for half in range(2):
        near_copy(True, half).start()
        near_copy(False, half).start()

    @pl.when(core == 0)
    def _():
        mate_copy(0, 0).start()
        mate_copy(0, 1).start()

    for copy in load_pool:
        copy.start()

    def slab(half):
        return slice(half * SLABS, (half + 1) * SLABS)

    for half in range(2):
        kall[seq * 2 + half] = own[0, slab(half)]
        vall[seq * 2 + half, :HD, :] = own[1, slab(half)].reshape(HALF, HD).T
    loads[7].wait()

    ones = jnp.ones((8, HD), jnp.bfloat16)
    own_k = own[0].reshape(TOK, HD)
    k_low, k_high = own_k[:HALF], own_k[HALF:]
    key_at = lax.broadcasted_iota(jnp.int32, (HALF, TOK), 0)
    query_at = lax.broadcasted_iota(jnp.int32, (HALF, TOK), 1)
    low_valid = key_at <= query_at
    high_valid = low_valid[:, :HALF]

    def query(head):
        return q_ref[0, :, head * HD:(head + 1) * HD]

    shifts = []
    for head in range(GROUP):
        product = (query(head).astype(jnp.float32) * own_k.astype(jnp.float32)).astype(jnp.bfloat16)
        shifts.append(dot_nt(ones, product)[:1])
    for head in range(GROUP):
        shift[head] = shifts[head]

    def own_scores(head):
        q = query(head)
        return dot_nt(k_low, q), dot_nt(k_high, q[HALF:])

    scores = own_scores(0)
    for head in range(GROUP):
        upcoming = own_scores(head + 1) if head + 1 < GROUP else None
        base = shift[head]
        low = jnp.where(low_valid, jnp.exp2((scores[0] - base) * SCALE), 0.0)
        high = jnp.where(high_valid, jnp.exp2((scores[1] - base[:, HALF:]) * SCALE), 0.0)
        first = dot_nn(vall[seq * 2], low.astype(jnp.bfloat16))
        second = dot_nn(vall[seq * 2 + 1], high.astype(jnp.bfloat16))
        acc[head, :, :HALF] = first[:, :HALF]
        acc[head, :, HALF:] = first[:, HALF:] + second
        scores = upcoming

    def attend(*taken):
        keys = jnp.concatenate([kall[index].reshape(HALF, HD) for index in taken], axis=0)
        values = jnp.concatenate([vall[index] for index in taken], axis=1)
        scores = dot_nt(keys, query(0))
        for head in range(GROUP):
            upcoming = dot_nt(keys, query(head + 1)) if head + 1 < GROUP else None
            weights = jnp.exp2((scores - shift[head]) * SCALE).astype(jnp.bfloat16)
            acc[head] += dot_nn(values, weights)
            scores = upcoming

    def take(kind, half):
        kall[held[kind] * 2 + half] = direct[kind][0, slab(half)]
        vall[held[kind] * 2 + half, :HD, :] = direct[kind][1, slab(half)].reshape(HALF, HD).T

    def arrive(kind, half):
        pltpu.make_async_remote_copy(
            src_ref=part(own, half), dst_ref=part(direct[kind], half),
            send_sem=rsend.at[half], recv_sem=drecv.at[kind, half],
            device_id=place(section, mate), device_id_type=MESH,
        ).wait_recv()
        if kind < 3:
            @pl.when(core == kind - 1)
            def _():
                relay_copy(kind == 1, half).start()

        @pl.when(origin[kind] < chip)
        def _():
            mate_copy(kind, half).start()
            take(kind, half)

    def fetch_table(kind):
        pltpu.make_async_remote_copy(
            src_ref=table0, dst_ref=tables[kind], send_sem=tsend.at[2], recv_sem=trecv.at[kind],
            device_id=place(section, mate), device_id_type=MESH,
        ).wait_recv()
        if kind < 3:
            @pl.when(core == kind - 1)
            def _():
                relay_table(kind == 1).start()
        local_owners(kind).start()

    def forward_pages(kind):
        local_owners(kind).wait()
        send_pages(kind)

    edge = chip == chips - 1
    turns = jnp.maximum(2 * chip, 2)
    visits = turns // 2

    def ready(turn, active):
        both = edge & (turn >= 0) & (turn < 4)
        single = jnp.where(turn < 0, 0, jnp.where(turn < 2, 1, 3))
        single = jnp.where(edge & (turn >= 4), 3, single)
        kinds = (jnp.where(both, 1, single), jnp.where(both, 2, single))
        halves = (jnp.where(both, turn // 2, 0), jnp.where(both, turn // 2, 1))
        straight = (turn >= 0) & (turn % 2 == 0)
        indices = []
        for kind, half in zip(kinds, halves):
            move = jnp.where(kind == 1, chips - 1, jnp.where(kind == 2, 1, jnp.where(kind == 3, 2, 0)))
            index = (lax.rem(chip + move, chips) * 2 + jnp.where(straight, core, 1 - core)) * 2 + half
            indices.append(index)

            @pl.when(active & jnp.logical_not(straight))
            def _():
                pltpu.make_async_remote_copy(
                    src_ref=part(own, 0), dst_ref=part(passed.at[kind], half),
                    send_sem=rsend.at[0], recv_sem=mrecv.at[kind, half],
                    device_id=place(section, mate), device_id_type=MESH,
                ).wait_recv()
                kall[index] = passed[kind, 0, pl.ds(half * SLABS, SLABS)]
                vall[index, :HD, :] = passed[kind, 1, pl.ds(half * SLABS, SLABS)].reshape(HALF, HD).T

        return indices

    @pl.loop(0, core + 1 + visits)
    def _(step):
        visit = step - core

        @pl.when(visit == 0)
        def _():
            send_pages(0)
            arrive(1, 0)
            arrive(2, 0)
            fetch_table(1)
            fetch_table(2)

        @pl.when(visit == jnp.where(edge, 1, 0))
        def _():
            arrive(1, 1)
            arrive(2, 1)
            forward_pages(1)
            forward_pages(2)

        @pl.when(visit == jnp.where(edge, 2, 1))
        def _():
            fetch_table(3)
            arrive(3, 0)
            arrive(3, 1)
            forward_pages(3)

        paired = (visit >= 1) & (visit < visits)
        turn = jnp.where(visit <= 0, visit, jnp.where(paired, 2 * visit - 1, turns - 1))
        wanted = (turn < 0) | (turn < 2 * chip)
        indices = ready(turn, wanted)

        @pl.when(wanted & jnp.logical_not(paired))
        def _():
            attend(*indices)

        @pl.when(paired)
        def _():
            after = turn + 1
            both = edge & (after < 4)
            kinds = (jnp.where(both, 1, 3), jnp.where(both, 2, 3))
            halves = (jnp.where(both, 1, 0), 1)
            more = []
            for kind, half in zip(kinds, halves):
                move = jnp.where(kind == 1, chips - 1, jnp.where(kind == 2, 1, 2))
                more.append((lax.rem(chip + move, chips) * 2 + core) * 2 + half)
            attend(*indices, *more)

    for head in range(GROUP):
        state = acc[head]
        total = state[HD:HD + 1]
        total_ref[head:head + 1, :] = total
        out_ref[0, :, head * HD:(head + 1) * HD] = (state[:HD] * (1.0 / total)).astype(jnp.bfloat16).T

    for up in (True, False):
        near_table(up).wait_send()
        for half in range(2):
            near_copy(up, half).wait_send()
    relay_table(True).wait_send()
    for half in range(2):
        relay_copy(True, half).wait_send()

        @pl.when(core == 0)
        def _():
            mate_copy(0, half).wait_send()

        for kind in (1, 2, 3):
            @pl.when(origin[kind] < chip)
            def _():
                mate_copy(kind, half).wait_send()

    for copy in load_pool:
        copy.wait()

    for kind in range(4):
        for offset in range(1, sections):
            for other in range(2):
                page_copy(kind, offset, other).wait_send()
        for other in range(2):
            @pl.when(core != other)
            def _():
                page_copy(kind, 0, other).wait_send()

    @pl.loop(0, sections)
    def _(row):
        @pl.loop(0, width)
        def _(far):
            @pl.when((row != section) | (far % 2 != core))
            def _():
                pltpu.make_async_remote_copy(
                    src_ref=outgoing.at[0, 0], dst_ref=pages.at[POOL + row * width + far],
                    send_sem=psend.at[0, 0], recv_sem=precv.at[row * width + far],
                    device_id=place(section, mate), device_id_type=MESH,
                ).wait_recv()


def prepare(sq_ref, sk_ref, sv_ref, q_all, new_part, new_v):
    for r in range(REQS):
        wide = sq_ref[r].astype(jnp.float32)
        q_all[r] = jnp.concatenate(
            [wide[:, h * HD:(h + 1) * HD] for h in range(GROUP)], axis=0
        ).astype(jnp.bfloat16)
    new_k = jnp.concatenate([sk_ref[r].astype(jnp.float32) for r in range(REQS)], 0).astype(jnp.bfloat16)
    new_v[...] = jnp.concatenate([sv_ref[r].astype(jnp.float32) for r in range(REQS)], 0).astype(jnp.bfloat16)
    new_scores = dot_nt(q_all[...].reshape(REQS * ROWS, HD), new_k)
    shape = (REQS * ROWS, REQS * STEPS)
    row = lax.broadcasted_iota(jnp.int32, shape, 0)
    column = lax.broadcasted_iota(jnp.int32, shape, 1)
    fits = (column // STEPS == row // ROWS) & (column % STEPS <= row % STEPS)
    new_part[...] = jnp.where(fits, new_scores, LOW).reshape(REQS, ROWS, REQS * STEPS)


def decode_kernel(
    table_hbm, length_hbm, pages, q_all, new_part, new_v, early_ref, total_ref,
    q_ref, karch_ref, varch_ref,
    final_ref, out_ref,
    table_ref, length_ref, sems, q_slow, k_slow, v_slow, o_slow,
):
    loads = [
        pltpu.make_async_copy(early_ref, final_ref, sems.at[0]),
        pltpu.make_async_copy(table_hbm, table_ref, sems.at[1]),
        pltpu.make_async_copy(length_hbm, length_ref, sems.at[2]),
    ]
    for copy in loads[1:]:
        copy.start()
    loads[0].start()
    for copy in loads[1:]:
        copy.wait()

    position = lax.broadcasted_iota(jnp.int32, (ROWS, CTX), 1)
    cut = 8

    def gather(r, b, low):
        return jnp.concatenate(
            [pages[table_ref[r, b * cut + i], low:low + PAGE] for i in range(cut)], axis=0
        )

    def score(r):
        q = q_all[r]
        parts = [dot_nt(q, gather(r, b, 0)) for b in range(MAXPG // cut)]
        return jnp.concatenate(parts, axis=1)

    def weigh(r, scores):
        scores = jnp.where(position < length_ref[r], scores, LOW)
        extra = new_part[r]
        top = jnp.maximum(jnp.max(scores, axis=1, keepdims=True), jnp.max(extra, axis=1, keepdims=True))
        weights = jnp.exp2((scores - top) * SCALE)
        extra = jnp.exp2((extra - top) * SCALE)
        total = jnp.sum(weights, axis=1, keepdims=True) + jnp.sum(extra, axis=1, keepdims=True)
        return weights.astype(jnp.bfloat16), extra.astype(jnp.bfloat16), total

    def combine(r, weights, extra, total):
        summed = dot_nn(extra, new_v[...])
        for b in range(MAXPG // cut):
            summed += dot_nn(weights[:, b * cut * PAGE:(b + 1) * cut * PAGE], gather(r, b, PAGE))
        result = summed / total
        out_ref[r] = jnp.concatenate(
            [result[h * STEPS:(h + 1) * STEPS] for h in range(GROUP)], axis=1
        ).astype(jnp.bfloat16)

    ahead = score(0)
    waiting = None
    for r in range(REQS):
        upcoming = score(r + 1) if r + 1 < REQS else None
        weighed = weigh(r, ahead)
        if waiting is not None:
            combine(r - 1, *waiting)
        waiting, ahead = weighed, upcoming
    combine(REQS - 1, *waiting)

    loads[0].wait()

    fine = jnp.min(jnp.where(total_ref[...] < LIMIT, 1.0, 0.0)) > 0.5

    @pl.when(jnp.logical_not(fine))
    def _():
        seq = lax.axis_index("seq")
        load = pltpu.make_async_copy(q_ref, q_slow, sems.at[0])
        load.start()
        load.wait()
        key_at = lax.broadcasted_iota(jnp.int32, (HALF, TOK), 0)
        query_at = lax.broadcasted_iota(jnp.int32, (HALF, TOK), 1)
        for head in range(GROUP):
            q = q_slow[0, :, head * HD:(head + 1) * HD]

            def advance(held, state):
                top, state_acc = state
                loads = (
                    pltpu.make_async_copy(karch_ref.at[held], k_slow, sems.at[1]),
                    pltpu.make_async_copy(varch_ref.at[held], v_slow, sems.at[2]),
                )
                for copy in loads:
                    copy.start()
                for copy in loads:
                    copy.wait()
                valid = key_at + held * HALF <= query_at + seq * TOK
                s = jnp.where(valid, dot_nt(k_slow[...].reshape(HALF, HD), q), LOW)
                fresh = jnp.maximum(top, jnp.max(s, axis=0, keepdims=True))
                w = jnp.exp2((s - fresh) * SCALE).astype(jnp.bfloat16)
                return fresh, state_acc * jnp.exp2((top - fresh) * SCALE) + dot_nn(v_slow[...], w)

            start = (jnp.full((1, TOK), LOW, jnp.float32), jnp.zeros((VROWS, TOK), jnp.float32))
            _, state = lax.fori_loop(0, 2 * seq + 2, advance, start)
            o_slow[0, :, head * HD:(head + 1) * HD] = (state[:HD] / state[HD:HD + 1]).astype(jnp.bfloat16).T
        store = pltpu.make_async_copy(o_slow, final_ref, sems.at[0])
        store.start()
        store.wait()


def in_hbm(array):
    return pltpu.with_memory_space_constraint(array, pltpu.HBM)


def on_device(
    prompt_query, prompt_keys, prompt_values, page_owner, pool_keys, pool_values,
    step_query, step_keys, step_values, page_table, context_len,
):
    sections = lax.axis_size("section")
    width = lax.axis_size("seq")
    count = sections * width
    chips = width // 2
    bf16, f32 = jnp.bfloat16, jnp.float32
    vmem = pl.BlockSpec(memory_space=pltpu.VMEM)
    hbm = pl.BlockSpec(memory_space=pltpu.HBM)
    anywhere = pl.BlockSpec(memory_space=pl.ANY)
    pages = TOK // PAGE
    dma = pltpu.SemaphoreType.DMA
    early, totals, karch, varch, held_pages, q_all, new_part, new_v = pl.pallas_call(
        functools.partial(prefill_kernel, chips, sections),
        out_shape=(
            jax.ShapeDtypeStruct((1, TOK, GROUP * HD), bf16),
            jax.ShapeDtypeStruct((GROUP, TOK), f32),
            jax.ShapeDtypeStruct((2 * width, SLABS, PAGE, HD), bf16),
            jax.ShapeDtypeStruct((2 * width, VROWS, HALF), bf16),
            jax.ShapeDtypeStruct((POOL + count, 2 * PAGE, HD), bf16),
            jax.ShapeDtypeStruct((REQS, ROWS, HD), bf16),
            jax.ShapeDtypeStruct((REQS, ROWS, REQS * STEPS), f32),
            jax.ShapeDtypeStruct((REQS * STEPS, HD), bf16),
        ),
        in_specs=[hbm] * 9,
        out_specs=(vmem,) * 8,
        scratch_shapes=[
            pltpu.VMEM((REQS, STEPS, GROUP * HD), bf16),
            pltpu.VMEM((REQS, STEPS, HD), bf16),
            pltpu.VMEM((REQS, STEPS, HD), bf16),
            pltpu.VMEM((1, TOK, GROUP * HD), bf16),
            *[pltpu.VMEM((2, pages, PAGE, HD), bf16)] * 4,
            pltpu.VMEM((4, 2, pages, PAGE, HD), bf16),
            *[pltpu.VMEM((1, pages), jnp.int32)] * 4,
            *[pltpu.SMEM((1, pages), jnp.int32)] * 4,
            pltpu.VMEM((GROUP, VROWS, TOK), f32),
            pltpu.VMEM((GROUP, 1, TOK), f32),
            pltpu.VMEM((4, 2 * sections, 2 * PAGE, HD), bf16),
            dma((2, 2)), dma((2,)), dma((4, 2)), dma((4, 2)), dma((4, 2)),
            dma((3,)), dma((4,)), dma((4, 2 * sections)), dma((count,)),
            dma((13,)),
        ],
        compiler_params=pltpu.CompilerParams(
            collective_id=0, has_side_effects=True, vmem_limit_bytes=32 * 2**20
        ),
        name="prefill",
    )(
        in_hbm(prompt_query),
        in_hbm(prompt_keys.reshape(pages, PAGE, HD)),
        in_hbm(prompt_values.reshape(pages, PAGE, HD)),
        in_hbm(page_owner),
        in_hbm(pool_keys),
        in_hbm(pool_values),
        in_hbm(step_query),
        in_hbm(step_keys),
        in_hbm(step_values),
    )
    return pl.pallas_call(
        decode_kernel,
        out_shape=(
            jax.ShapeDtypeStruct((1, TOK, GROUP * HD), bf16),
            jax.ShapeDtypeStruct((REQS, STEPS, GROUP * HD), bf16),
        ),
        in_specs=[hbm] * 2 + [vmem] * 4 + [anywhere, vmem, hbm, anywhere, anywhere],
        out_specs=(hbm, vmem),
        scratch_shapes=[
            pltpu.SMEM((REQS, MAXPG), jnp.int32),
            pltpu.SMEM((REQS,), jnp.int32),
            dma((3,)),
            pltpu.VMEM((1, TOK, GROUP * HD), bf16),
            pltpu.VMEM((SLABS, PAGE, HD), bf16),
            pltpu.VMEM((VROWS, HALF), bf16),
            pltpu.VMEM((1, TOK, GROUP * HD), bf16),
        ],
        compiler_params=pltpu.CompilerParams(vmem_limit_bytes=32 * 2**20),
        name="decode",
    )(
        in_hbm(page_table), in_hbm(context_len), held_pages, q_all, new_part, new_v,
        early, totals, in_hbm(prompt_query), karch, varch,
    )


def solution(mesh):
    in_specs = (
        P("section", "seq", "tensor"),
        P("section", "seq", "tensor"),
        P("section", "seq", "tensor"),
        P("section", "seq"),
        P(("section", "seq"), None, "tensor"),
        P(("section", "seq"), None, "tensor"),
        P(("section", "seq"), None, "tensor"),
        P(("section", "seq"), None, "tensor"),
        P(("section", "seq"), None, "tensor"),
        P(("section", "seq"), None),
        P(("section", "seq")),
    )
    out_specs = (P("section", "seq", "tensor"), P(("section", "seq"), None, "tensor"))
    return jax.shard_map(
        on_device, mesh=mesh, in_specs=in_specs, out_specs=out_specs, check_vma=False
    )
```
